256 devices in a mesh: dp: 4 (over z_lo), cls: 64 (over y, z_hi, x, core).
Axes of the slice: x: 4, y: 4, z: 8 (z_hi: 2, z_lo: 4; z = z_hi * 4 + z_lo), core: 2. Of those that a mesh axis runs over, the one named last changes fastest.
Arguments:
- embeddings: bfloat16 [4096, 384], P(('dp', 'cls')), may hold values from -4 to 4
- cluster_ids: int32 [4096], P(('dp', 'cls')), may hold values from 0 to 131071
- prototypes: bfloat16 [384, 131072], P(None, 'cls'), may hold values from -2 to 2
Outputs:
- embed_grad: float32 [4096, 384], P(('dp', 'cls'))
- proto_grad: float32 [384, 131072], P('dp', 'cls')
The draws below stay inside these ranges and needn't reach their ends.
All inputs are finite; a program needn't handle non-finite values.
Results may differ from the reference program's by a relative error of at most 0.00505.
Values may be sent and summed in bfloat16 or wider, within the bound.
A program may use at most 128 MiB of HBM per device.

```python
import math
import jax
import jax.numpy as jnp
from jax import lax

D = 384
K = 131072
CROPS = 4096
N_CLS = 64


def shaped_noise(raw):
    return raw


def proto_table(key):
    key_normal, key_scale = jax.random.split(jax.random.fold_in(key, 101), 2)
    amplitude = math.sqrt(0.3 / math.sqrt(D))
    raw = jnp.clip(jax.random.normal(key_normal, (D, K), dtype=jnp.float32), -5.0, 5.0)
    base = shaped_noise(raw)
    column_scale = jnp.exp(jax.random.uniform(key_scale, (K,), jnp.float32, -0.58, 0.58))
    anchors = jnp.arange(8, dtype=jnp.int32) * (K // 8) + 5
    column_scale = column_scale.at[anchors].set(column_scale[anchors])
    table = amplitude * base * column_scale[None, :]
    table = table.at[:, anchors + 1].set(table[:, anchors + 1])
    return table


def draw_prototypes(key, part):
    table = proto_table(key)
    return table.astype(jnp.bfloat16)


def draw_embeddings(key, part):
    key = jax.random.fold_in(key, 7)
    key_rows, key_scale = jax.random.split(key, 2)
    amplitude = math.sqrt(0.3 / math.sqrt(D))
    raw = jnp.clip(jax.random.normal(key_rows, (CROPS, D), dtype=jnp.float32), -5.0, 5.0)
    base = shaped_noise(raw)
    row_scale = jnp.exp(jax.random.uniform(key_scale, (CROPS,), jnp.float32, -1.15, 1.15))
    rows = amplitude * base * row_scale[:, None]
    positions = jnp.arange(8, dtype=jnp.int32) * (CROPS // 8) + 3
    rows = rows.at[positions].set(rows[positions])
    return rows.astype(jnp.bfloat16)


def with_ends(values, rng, smallest, high):
    longest = values.shape.index(max(values.shape))
    spots = []
    for shift in (0, 1):
        where = [jax.random.randint(jax.random.fold_in(rng, axis), (), 0, length) for axis, length in enumerate(values.shape)]
        where[longest] = (where[longest] + shift) % values.shape[longest]
        spots.append(tuple(where))
    return values.at[spots[0]].set(smallest).at[spots[1]].set(high)


def setup_inputs(seed: int = 0) -> dict:
    key_list = jax.random.split(jax.random.key(seed), 4)
    embeddings = draw_embeddings(jax.random.fold_in(key_list[3], 71), 0)
    cluster_ids = with_ends(jax.random.randint(key_list[1], (CROPS,), 0, K), jax.random.fold_in(key_list[1], 1), 0, K - 1).astype(jnp.int32)
    prototypes = draw_prototypes(jax.random.fold_in(key_list[3], 71), 0)
    return dict(embeddings=embeddings, cluster_ids=cluster_ids, prototypes=prototypes)


LOGIT_SCALE = 10.0


def reference(embeddings, cluster_ids, prototypes):
    width = K // N_CLS
    indices = jnp.arange(N_CLS, dtype=jnp.int32)
    contract_cols = (((1,), (1,)), ((), ()))
    contract_rows = (((0,), (0,)), ((), ()))

    def block_logits(index):
        weights = lax.dynamic_slice_in_dim(prototypes, index * width, width, 1)
        logits = jnp.dot(embeddings, weights, preferred_element_type=jnp.float32) * LOGIT_SCALE
        return logits, weights

    def stats_step(carry, index):
        row_peak, row_total = carry
        logits, unused = block_logits(index)
        new_peak = jnp.maximum(row_peak, jnp.max(logits, axis=1))
        row_total = row_total * jnp.exp(row_peak - new_peak) + jnp.sum(jnp.exp(logits - new_peak[:, None]), axis=1)
        return (new_peak, row_total), None

    start_carry = (jnp.full((CROPS,), -jnp.inf, dtype=jnp.float32), jnp.zeros((CROPS,), dtype=jnp.float32))
    (row_peak, row_total), unused = lax.scan(stats_step, start_carry, indices)

    def block_probs(index):
        logits, weights = block_logits(index)
        return jnp.exp(logits - row_peak[:, None]) / row_total[:, None], weights

    column_mass = lax.map(lambda index: jnp.sum(block_probs(index)[0], axis=0), indices)
    log_ratio = jnp.log(column_mass * (K / CROPS))

    def dot_step(carry, index):
        soft_probs, unused_weights = block_probs(index)
        return carry + jnp.sum(soft_probs * log_ratio[index][None, :], axis=1), None

    row_dot, unused = lax.scan(dot_step, jnp.zeros((CROPS,), dtype=jnp.float32), indices)

    def grad_step(carry, index):
        soft_probs, weights = block_probs(index)
        columns = index * width + jnp.arange(width, dtype=jnp.int32)
        onehot = (cluster_ids[:, None] == columns[None, :]).astype(jnp.float32)
        grad_logit = soft_probs - onehot + soft_probs * (log_ratio[index][None, :] - row_dot[:, None])
        grad_narrow = grad_logit.astype(jnp.bfloat16)
        carry = carry + lax.dot_general(grad_narrow, weights, contract_cols, preferred_element_type=jnp.float32) * LOGIT_SCALE
        proto_block = lax.dot_general(embeddings, grad_narrow, contract_rows, preferred_element_type=jnp.float32) * LOGIT_SCALE
        return carry, proto_block

    embed_grad, proto_blocks = lax.scan(grad_step, jnp.zeros((CROPS, D), dtype=jnp.float32), indices)
    proto_grad = jnp.moveaxis(proto_blocks, 0, 1).reshape(D, K)
    return embed_grad, proto_grad
```

```python
import functools

import jax
import jax.numpy as jnp
from jax import lax
from jax.experimental import pallas as pl
from jax.experimental.pallas import tpu as pltpu
from jax.sharding import PartitionSpec as P

LOGIT_SCALE = 10.0
MESH = pl.DeviceIdType.MESH
F32 = jnp.float32
BF16 = jnp.bfloat16

D = 384
DX = 512
W = 2048
R = 1024
NC = 4
CW = W // NC
Q = D // 4
NT = (((1,), (1,)), ((), ()))
SEVEN = [(dz, da) for da in range(4) for dz in range(2) if dz or da]


def split_rows(v):
    hi = v.astype(BF16)
    r1 = v - hi.astype(F32)
    mid = r1.astype(BF16)
    lo = (r1 - mid.astype(F32)).astype(BF16)
    row = lax.broadcasted_iota(jnp.int32, (16, v.shape[1]), 0)
    zero = jnp.zeros((16, v.shape[1]), F32)
    out = jnp.where(row == 0, hi.astype(F32), zero)
    out = jnp.where(row == 1, mid.astype(F32), out)
    out = jnp.where(row == 2, lo.astype(F32), out)
    return out.astype(BF16)


def kernel(classes_over_crops, e_ref, id_ref, w_ref, eo_ref, po_ref,
           eg, pb, lb, mcol, scol, acol, ccol, icol, et, gb,
           st, ra, rb, rc, cm, qt, qa, qb, qc, pf, pp, pr,
           xe, xc, y1, xb, y2, xa,
           s_e1, r_e1, s_e2, r_e2, s_e3, r_e3,
           s_a, r_a, s_b, r_b, s_c, r_c, s_m, r_m,
           s_p, r_p, s_x1, r_x1, s_x2, r_x2, s_x3, r_x3):
    dp = lax.axis_index("dp")
    cls = lax.axis_index("cls")
    core = lax.rem(cls, 2)
    x = lax.rem(cls // 2, 4)
    zh = lax.rem(cls // 8, 2)
    y = cls // 16
    other = 1 - core
    alpha = y * other + x * core
    beta = x * other + y * core

    def at(zz, aa, bb):
        yy = aa * other + bb * core
        xx = bb * other + aa * core
        return (dp, ((yy * 2 + zz) * 4 + xx) * 2 + core)

    def add4(v, k):
        return lax.rem(v + k, 4)

    def seven(dz, da):
        return lax.rem(zh + dz, 2), add4(alpha, da)

    partner = (dp, cls + 1 - 2 * core)
    dp_peers = [(add4(dp, j), cls) for j in (1, 2, 3)]
    beta_peers = [at(zh, alpha, add4(beta, k)) for k in (1, 2, 3)]
    seven_peers = [at(*seven(dz, da), beta) for dz, da in SEVEN]

    barrier = pltpu.get_barrier_semaphore()
    everyone = [partner] + dp_peers + beta_peers + seven_peers
    for peer in everyone:
        pl.semaphore_signal(barrier, inc=1, device_id=peer, device_id_type=MESH)

    ids = id_ref[...]
    lane = lax.broadcasted_iota(jnp.int32, (16, 128), 1)
    digits = jnp.where(lane == 0, ids >> 10, jnp.where(lane == 1, (ids >> 5) & 31, jnp.where(lane == 2, ids & 31, 0)))
    eg[core, beta, zh, alpha, :, :D] = e_ref[...]
    eg[core, beta, zh, alpha, :, D:] = digits.astype(F32).astype(BF16)

    pl.semaphore_wait(barrier, len(everyone))

    def remote(src, dst, ssem, rsem, peer):
        return pltpu.make_async_remote_copy(
            src_ref=src, dst_ref=dst, send_sem=ssem, recv_sem=rsem, device_id=peer, device_id_type=MESH
        )

    mine = eg.at[core, beta, zh, alpha]
    sends = []
    for j, peer in enumerate(seven_peers):
        c = remote(mine, mine, s_e1.at[j], r_e1.at[j], peer)
        c.start()
        sends.append(c)
    for j, (dz, da) in enumerate(SEVEN):
        block = eg.at[core, beta, lax.rem(zh + dz, 2), add4(alpha, 4 - da)]
        remote(block, block, s_e1.at[j], r_e1.at[j], seven_peers[j]).wait_recv()
    row = eg.at[core, beta]
    for k, peer in enumerate(beta_peers):
        c = remote(row, row, s_e2.at[k], r_e2.at[k], peer)
        c.start()
        sends.append(c)
    c = remote(row, row, s_e3.at[0], r_e3.at[0], partner)
    c.start()
    sends.append(c)
    for k in (1, 3, 2):
        block = eg.at[core, add4(beta, 4 - k)]
        remote(block, block, s_e2.at[k - 1], r_e2.at[k - 1], beta_peers[k - 1]).wait_recv()
        c = remote(block, block, s_e3.at[k], r_e3.at[k], partner)
        c.start()
        sends.append(c)

    def half_logits(ci):
        rows = eg[ci].reshape(R // 2, DX)
        left = rows[:, :D]

        def tile(t, _):
            cols = pl.ds(pl.multiple_of(t * CW, CW), CW)
            lb[:, cols] = jnp.dot(left, w_ref[:, cols], preferred_element_type=F32)
            return 0

        lax.fori_loop(0, W // CW, tile, 0)
        base = ci * (R // 2)

        def strip(i, _):
            here = pl.ds(pl.multiple_of(i * 32, 32), 32)
            there = pl.ds(pl.multiple_of(base + i * 32, 32), 32)
            v = lb[here, :] * LOGIT_SCALE
            m = jnp.max(v, axis=1, keepdims=True)
            p = jnp.exp(v - m)
            s = jnp.sum(p, axis=1, keepdims=True)
            pb[there, :] = p.astype(BF16)
            mcol[there, :] = jnp.broadcast_to(m, (32, 128))
            scol[there, :] = jnp.broadcast_to(s, (32, 128))
            return 0

        lax.fori_loop(0, R // 64, strip, 0)

    half_logits(core)
    obeta = alpha
    for k in (0, 1, 3, 2):
        block = eg.at[other, add4(obeta, 4 - k)]
        remote(block, block, s_e3.at[k], r_e3.at[k], partner).wait_recv()
    half_logits(other)
    for i in range(8):
        here = pl.ds(i * 128, 128)
        st[0, i : i + 1, :] = mcol[here, :].T[0:1, :]
        st[0, 8 + i : 9 + i, :] = scol[here, :].T[0:1, :]
    m_own = st[0, 0:8, :]

    def exchange(src, dst, ssem, rsem, peers):
        cs = [remote(src, dst.at[j], ssem.at[j], rsem.at[j], peer) for j, peer in enumerate(peers)]
        for c in cs:
            c.start()
        return cs

    def merge(src, dst, n):
        m = src[0:8, :]
        for j in range(n):
            m = jnp.maximum(m, dst[j, 0:8, :])
        s = src[8:16, :] * jnp.exp(src[0:8, :] - m)
        for j in range(n):
            s = s + dst[j, 8:16, :] * jnp.exp(dst[j, 0:8, :] - m)
        return m, s

    cs = exchange(st.at[0], ra, s_a.at[0], r_a.at[0], seven_peers)

    for ci in range(2):
        for b in range(4):
            blk = eg[ci, b].reshape(128, DX)
            at_row = (ci * 4 + b) * 128
            et[:, at_row : at_row + 128] = blk[:, :D].T
            d = blk[:, D:].astype(F32)
            icol[at_row : at_row + 128, :] = jnp.broadcast_to(
                d[:, 0:1] * 1024.0 + d[:, 1:2] * 32.0 + d[:, 2:3], (128, 128)
            )
    for c in cs:
        c.wait()
    m, s = merge(st.at[0], ra, 7)
    st[1, 0:8, :] = m
    st[1, 8:16, :] = s
    for c in (cs := exchange(st.at[1], rb, s_b.at[0], r_b.at[0], beta_peers)):
        c.wait()
    m, s = merge(st.at[1], rb, 3)
    st[2, 0:8, :] = m
    st[2, 8:16, :] = s
    for c in (cs := exchange(st.at[2], rc, s_c.at[0], r_c.at[0], [partner])):
        c.wait()
    m, s = merge(st.at[2], rc, 1)
    f = jnp.exp(m_own - m) / s

    frow = jnp.concatenate([f[i : i + 1, :] for i in range(8)], axis=1)
    fs = split_rows(frow)

    def mass(t, _):
        cols = pl.ds(pl.multiple_of(t * CW, CW), CW)
        part = jnp.dot(fs, pb[:, cols], preferred_element_type=F32)
        cm[0, :, cols] = jnp.sum(part, axis=0, keepdims=True)
        return 0

    lax.fori_loop(0, W // CW, mass, 0)
    cs = [remote(cm.at[0], cm.at[j], s_m.at[j - 1], r_m.at[j - 1], dp_peers[j - 1]) for j in (1, 2, 3)]
    for c in cs:
        c.start()
    for i in range(8):
        acol[i * 128 : (i + 1) * 128, :] = jnp.broadcast_to(f[i : i + 1, :], (128, 128)).T
    for c in cs:
        c.wait()
    lr = jnp.log((cm[0] + cm[1] + cm[2] + cm[3]) * classes_over_crops)

    ls = split_rows(lr)
    for h in range(2):
        part = lax.dot_general(ls, pb[h * 512 : (h + 1) * 512, :], NT, preferred_element_type=F32)
        part = jnp.sum(part, axis=0, keepdims=True)
        for i in range(4):
            k = h * 4 + i
            qt[0, k : k + 1, :] = part[:, i * 128 : (i + 1) * 128] * f[k : k + 1, :]
    for c in (cs := exchange(qt.at[0], qa, s_a.at[1], r_a.at[1], seven_peers)):
        c.wait()
    qt[1] = qt[0] + ((qa[0] + qa[1]) + (qa[2] + qa[3])) + ((qa[4] + qa[5]) + qa[6])
    for c in (cs := exchange(qt.at[1], qb, s_b.at[1], r_b.at[1], beta_peers)):
        c.wait()
    qt[2] = qt[1] + ((qb[0] + qb[1]) + qb[2])
    for c in (cs := exchange(qt.at[2], qc, s_c.at[1], r_c.at[1], [partner])):
        c.wait()
    rd = qt[2] + qc[0]
    cc = f * (1.0 - rd)
    for i in range(8):
        ccol[i * 128 : (i + 1) * 128, :] = jnp.broadcast_to(cc[i : i + 1, :], (128, 128)).T

    first_col = cls * W

    def chunk(t, _):
        cols = pl.ds(pl.multiple_of(t * CW, CW), CW)
        lrc = jnp.log((cm[0, :, cols] + cm[1, :, cols] + cm[2, :, cols] + cm[3, :, cols]) * classes_over_crops)
        ramp = (lax.broadcasted_iota(jnp.int32, (1, CW), 1) + (first_col + t * CW)).astype(F32)

        def strip(i, _):
            rows = pl.ds(pl.multiple_of(i * 32, 32), 32)
            a = acol[rows, 0:1]
            c = ccol[rows, 0:1]
            g = pb[rows, cols].astype(F32) * (a * lrc + c)
            g = g - (icol[rows, 0:1] == ramp).astype(F32)
            gb[rows, cols] = g.astype(BF16)
            return 0

        lax.fori_loop(0, R // 32, strip, 0)
        part = jnp.dot(et[...], gb[:, cols], preferred_element_type=F32) * LOGIT_SCALE
        for k in range(4):
            pf[t, k] = part[k * Q : (k + 1) * Q, :]
            pp[t, k] = part[k * Q : (k + 1) * Q, :].astype(BF16)
        for j in (1, 2, 3):
            remote(pp.at[t, add4(dp, j)], pr.at[t, j - 1], s_p.at[t, j - 1], r_p.at[t, j - 1], dp_peers[j - 1]).start()
        return 0

    lax.fori_loop(0, NC, chunk, 0)

    def half_embed(ci):
        def piece(b, _):
            rows = pl.ds(pl.multiple_of((ci * 4 + b) * 128, 128), 128)
            v = lax.dot_general(gb[rows, :], w_ref[...], NT, preferred_element_type=F32) * LOGIT_SCALE
            xe[ci, b] = v.reshape(2, 4, 16, D)
            return 0

        lax.fori_loop(0, 4, piece, 0)

    half_embed(other)
    c1 = remote(xe.at[other], xc, s_x1, r_x1, partner)
    c1.start()
    half_embed(core)
    c1.wait()
    xe[core] = xe[core] + xc[...]
    y1[...] = xe[core].astype(BF16)
    cs = [
        remote(y1.at[add4(beta, k)], xb.at[k - 1], s_x2.at[k - 1], r_x2.at[k - 1], beta_peers[k - 1])
        for k in (1, 2, 3)
    ]
    for c in cs:
        c.start()
    for c in cs:
        c.wait()
    own = xe[core, beta] + xb[0].astype(F32) + xb[1].astype(F32) + xb[2].astype(F32)
    xe[core, beta] = own
    y2[...] = own.astype(BF16)
    cs = []
    for j, (dz, da) in enumerate(SEVEN):
        z2, a2 = seven(dz, da)
        cs.append(remote(y2.at[z2, a2], xa.at[j], s_x3.at[j], r_x3.at[j], seven_peers[j]))
    for c in cs:
        c.start()

    for t in range(NC):
        for j in (1, 2, 3):
            remote(pp.at[t, add4(dp, j)], pr.at[t, j - 1], s_p.at[t, j - 1], r_p.at[t, j - 1], dp_peers[j - 1]).wait()
        po_ref[:, t * CW : (t + 1) * CW] = pf[t, dp] + (
            pr[t, 0].astype(F32) + pr[t, 1].astype(F32) + pr[t, 2].astype(F32)
        )
    for c in cs:
        c.wait()
    total = xe[core, beta, zh, alpha]
    for j in range(7):
        total = total + xa[j].astype(F32)
    eo_ref[...] = total
    for c in sends:
        c.wait_send()


def on_device(classes_over_crops, embeddings, cluster_ids, prototypes):
    vmem = pl.BlockSpec(memory_space=pltpu.VMEM)
    dma = pltpu.SemaphoreType.DMA
    V = pltpu.VMEM
    scratch = [
        V((2, 4, 2, 4, 16, DX), BF16),
        V((R, W), BF16),
        V((R // 2, W), F32),
        V((R, 128), F32),
        V((R, 128), F32),
        V((R, 128), F32),
        V((R, 128), F32),
        V((R, 128), F32),
        V((D, R), BF16),
        V((R, W), BF16),
        V((3, 16, 128), F32),
        V((7, 16, 128), F32),
        V((3, 16, 128), F32),
        V((1, 16, 128), F32),
        V((4, 1, W), F32),
        V((3, 8, 128), F32),
        V((7, 8, 128), F32),
        V((3, 8, 128), F32),
        V((1, 8, 128), F32),
        V((NC, 4, Q, CW), F32),
        V((NC, 4, Q, CW), BF16),
        V((NC, 3, Q, CW), BF16),
        V((2, 4, 2, 4, 16, D), F32),
        V((4, 2, 4, 16, D), F32),
        V((4, 2, 4, 16, D), BF16),
        V((3, 2, 4, 16, D), BF16),
        V((2, 4, 16, D), BF16),
        V((7, 16, D), BF16),
        dma((7,)), dma((7,)), dma((3,)), dma((3,)), dma((4,)), dma((4,)),
        dma((2, 7)), dma((2, 7)), dma((2, 3)), dma((2, 3)), dma((2, 1)), dma((2, 1)),
        dma((3,)), dma((3,)),
        dma((NC, 3)), dma((NC, 3)),
        dma, dma, dma((3,)), dma((3,)), dma((7,)), dma((7,)),
    ]
    return pl.pallas_call(
        functools.partial(kernel, classes_over_crops),
        out_shape=(jax.ShapeDtypeStruct((16, D), F32), jax.ShapeDtypeStruct((Q, W), F32)),
        in_specs=[vmem] * 3,
        out_specs=(vmem, vmem),
        scratch_shapes=scratch,
        compiler_params=pltpu.CompilerParams(
            collective_id=0, has_side_effects=True, vmem_limit_bytes=56 * 2**20
        ),
    )(embeddings, cluster_ids.reshape(16, 1), prototypes)


def solution(mesh):
    placed = (P(("dp", "cls"), None), P(("dp", "cls")), P(None, "cls"))
    return jax.shard_map(
        functools.partial(on_device, 131072 / 4096),
        mesh=mesh,
        in_specs=placed,
        out_specs=(P(("dp", "cls"), None), P("dp", "cls")),
        check_vma=False,
    )
```

```python
import functools

import jax
import jax.numpy as jnp
from jax import lax
from jax.experimental import pallas as pl
from jax.experimental.pallas import tpu as pltpu
from jax.sharding import PartitionSpec as P

LOGIT_SCALE = 10.0
MESH = pl.DeviceIdType.MESH
F32 = jnp.float32
BF16 = jnp.bfloat16

D = 384
DX = 512
W = 2048
R = 1024
H = W // 2
NC = 4
CW = H // NC
Q = D // 4
NT = (((1,), (1,)), ((), ()))
SEVEN = [(dz, da) for da in range(4) for dz in range(2) if dz or da]


def split_rows(v):
    hi = v.astype(BF16)
    r1 = v - hi.astype(F32)
    mid = r1.astype(BF16)
    lo = (r1 - mid.astype(F32)).astype(BF16)
    row = lax.broadcasted_iota(jnp.int32, (16, v.shape[1]), 0)
    zero = jnp.zeros((16, v.shape[1]), F32)
    out = jnp.where(row == 0, hi.astype(F32), zero)
    out = jnp.where(row == 1, mid.astype(F32), out)
    out = jnp.where(row == 2, lo.astype(F32), out)
    return out.astype(BF16)


def kernel(classes_over_crops, id_ref, e_ref, w_hbm, eo_ref, po_ref,
           w_ref, eg, eg2, pb, lb2, pb2, mcol, scol, acol, ccol, icol, acol2, ccol2, icol2, mcol2, et, et2, gb, gb2,
           st, ra, rb, rc, cm, lrow, lhalf, qt, qa, qb, qc, pf, pp, pr, ps, po2,
           xe, xc, y1, xb, y2, xa,
           s_w, s_e1, r_e1, s_e2, r_e2, s_e3, r_e3, s_f1, r_f1, s_f2, r_f2, s_f3, r_f3,
           s_a, r_a, s_b, r_b, s_c, r_c, s_m, r_m,
           s_po, r_po, s_pi, r_pi, s_ps, r_ps, s_x1, r_x1, s_x2, r_x2, s_x3, r_x3):
    dp = lax.axis_index("dp")
    cls = lax.axis_index("cls")
    core = lax.rem(cls, 2)
    x = lax.rem(cls // 2, 4)
    zh = lax.rem(cls // 8, 2)
    y = cls // 16
    other = 1 - core
    alpha = y * other + x * core
    beta = x * other + y * core
    pair = dp // 2
    mate = dp + 1 - 2 * lax.rem(dp, 2)
    inner = jnp.logical_or(dp == 1, dp == 2)
    far_in = 2 - pair
    far_out = 3 - 3 * pair
    own_cols = pair * H

    def at(zz, aa, bb):
        yy = aa * other + bb * core
        xx = bb * other + aa * core
        return (dp, ((yy * 2 + zz) * 4 + xx) * 2 + core)

    def add4(v, k):
        return lax.rem(v + k, 4)

    def seven(dz, da):
        return lax.rem(zh + dz, 2), add4(alpha, da)

    twin = cls + 1 - 2 * core
    partner = (dp, twin)
    buddy = add4(dp, 2)
    mate_peer = (mate, cls)
    pair_peers = [partner, (buddy, cls), (buddy, twin)]
    dp_peers = [(add4(dp, j), cls) for j in (1, 2, 3)]
    beta_peers = [at(zh, alpha, add4(beta, k)) for k in (1, 2, 3)]
    seven_peers = [at(*seven(dz, da), beta) for dz, da in SEVEN]

    barrier = pltpu.get_barrier_semaphore()
    everyone = [partner, (buddy, twin)] + dp_peers + beta_peers + seven_peers
    for peer in everyone:
        pl.semaphore_signal(barrier, inc=1, device_id=peer, device_id_type=MESH)
    load = pltpu.make_async_copy(w_hbm, w_ref, s_w)
    load.start()

    lane = lax.broadcasted_iota(jnp.int32, (16, 128), 1)
    line = lax.broadcasted_iota(jnp.int32, (16, 128), 0)
    ids = jnp.zeros((16, 128), jnp.int32)
    for i in range(16):
        ids = jnp.where(line == i, id_ref[i], ids)
    digits = jnp.where(lane == 0, ids >> 10, jnp.where(lane == 1, (ids >> 5) & 31, jnp.where(lane == 2, ids & 31, 0)))
    eg[core, beta, zh, alpha, :, :D] = e_ref[...]
    eg[core, beta, zh, alpha, :, D:] = digits.astype(F32).astype(BF16)

    pl.semaphore_wait(barrier, len(everyone))

    def remote(src, dst, ssem, rsem, peer):
        return pltpu.make_async_remote_copy(
            src_ref=src, dst_ref=dst, send_sem=ssem, recv_sem=rsem, device_id=peer, device_id_type=MESH
        )

    sends = []

    def post(src, dst, ssem, rsem, peer):
        c = remote(src, dst, ssem, rsem, peer)
        c.start()
        sends.append(c)

    mine = eg.at[core, beta, zh, alpha]
    for j, peer in enumerate(seven_peers):
        post(mine, mine, s_e1.at[j], r_e1.at[j], peer)
    for j, (dz, da) in enumerate(SEVEN):
        block = eg.at[core, beta, lax.rem(zh + dz, 2), add4(alpha, 4 - da)]
        remote(block, block, s_e1.at[j], r_e1.at[j], seven_peers[j]).wait_recv()
    row = eg.at[core, beta]
    for k, peer in enumerate(beta_peers):
        post(row, row, s_e2.at[k], r_e2.at[k], peer)
    post(row, row, s_e3.at[0], r_e3.at[0], partner)
    row2 = eg2.at[core, beta]
    post(row, row2, s_f1, r_f1, pair_peers[1])
    load.wait()
    for k in (1, 3, 2):
        b = add4(beta, 4 - k)
        block = eg.at[core, b]
        remote(block, block, s_e2.at[k - 1], r_e2.at[k - 1], beta_peers[k - 1]).wait_recv()
        post(block, block, s_e3.at[k], r_e3.at[k], partner)

    def half_logits(ci):
        for h in range(2):
            left = eg[ci, 2 * h : 2 * h + 2].reshape(256, DX)[:, :D]
            there = pl.ds(pl.multiple_of(ci * (R // 2) + h * 256, 256), 256)
            v = jnp.dot(left, w_ref[...], preferred_element_type=F32) * LOGIT_SCALE
            m = jnp.max(v, axis=1, keepdims=True)
            p = jnp.exp(v - m)
            s = jnp.sum(p, axis=1, keepdims=True)
            pb[there, :] = p.astype(BF16)
            mcol[there, :] = jnp.broadcast_to(m, (256, 128))
            scol[there, :] = jnp.broadcast_to(s, (256, 128))

    half_logits(core)
    for k in (0, 1, 3, 2):
        block = eg.at[other, add4(alpha, 4 - k)]
        remote(block, block, s_e3.at[k], r_e3.at[k], partner).wait_recv()
    half_logits(other)

    remote(row2, row2, s_f1, r_f1, pair_peers[1]).wait_recv()
    for k, peer in enumerate(beta_peers):
        post(row2, row2, s_f2.at[k], r_f2.at[k], peer)
    post(row2, row2, s_f3.at[0], r_f3.at[0], partner)

    eye = lax.broadcasted_iota(jnp.int32, (128, 128), 0) == lax.broadcasted_iota(jnp.int32, (128, 128), 1)

    def to_line(cols):
        return jnp.sum(jnp.where(eye, cols, 0.0), axis=0, keepdims=True)

    def to_cols(dst, lines):
        for i in range(8):
            dst[i * 128 : (i + 1) * 128, :] = jnp.broadcast_to(lines[i : i + 1, :], (128, 128)).T

    for i in range(8):
        here = pl.ds(i * 128, 128)
        st[0, i : i + 1, :] = to_line(mcol[here, :])
        st[0, 8 + i : 9 + i, :] = to_line(scol[here, :])

    def exchange(src, dst, ssem, rsem, peers):
        cs = [remote(src, dst.at[j], ssem.at[j], rsem.at[j], peer) for j, peer in enumerate(peers)]
        for c in cs:
            c.start()
        return cs

    def merge(parts):
        m = parts[0][0:8, :]
        for v in parts[1:]:
            m = jnp.maximum(m, v[0:8, :])
        s = parts[0][8:16, :] * jnp.exp(parts[0][0:8, :] - m)
        for v in parts[1:]:
            s = s + v[8:16, :] * jnp.exp(v[0:8, :] - m)
        return m, s

    cs = exchange(st.at[0], ra, s_a.at[0], r_a.at[0], seven_peers)

    for k in (1, 3, 2):
        block = eg2.at[core, add4(beta, 4 - k)]
        remote(block, block, s_f2.at[k - 1], r_f2.at[k - 1], beta_peers[k - 1]).wait_recv()
        post(block, block, s_f3.at[k], r_f3.at[k], partner)

    first_col = (cls * W).astype(F32)
    drow = lax.broadcasted_iota(jnp.int32, (128, 128), 0)
    weigh = jnp.where(drow == 0, 1024.0, jnp.where(drow == 1, 32.0, jnp.where(drow == 2, 1.0, 0.0))).astype(BF16)
    ramp = lax.broadcasted_iota(jnp.int32, (1, 128), 1).astype(F32)

    def turn(src, dst_t, dst_i, base):
        rows = src[...].reshape(R, DX)
        for i in range(8):
            dst_t[:, i * 128 : (i + 1) * 128] = rows[i * 128 : (i + 1) * 128, :D].T
        dst_i[...] = jnp.dot(rows[:, D:], weigh, preferred_element_type=F32) - (ramp + base)

    turn(eg, et, icol, first_col)
    for c in cs:
        c.wait()
    m, s = merge([st[0]] + [ra[j] for j in range(7)])
    st[1, 0:8, :] = m
    st[1, 8:16, :] = s
    cs = exchange(st.at[1], rb, s_b.at[0], r_b.at[0], beta_peers)

    for k in (0, 1, 3, 2):
        block = eg2.at[other, add4(alpha, 4 - k)]
        remote(block, block, s_f3.at[k], r_f3.at[k], partner).wait_recv()
    half_w = pl.ds(pl.multiple_of(own_cols, H), H)
    for h in range(2):
        left = eg2[h].reshape(R // 2, DX)[:, :D]
        lb2[h * 512 : (h + 1) * 512, :] = jnp.dot(left, w_ref[:, half_w], preferred_element_type=F32) * LOGIT_SCALE
    for c in cs:
        c.wait()
    m, s = merge([st[1]] + [rb[j] for j in range(3)])
    st[2, 0:8, :] = m
    st[2, 8:16, :] = s
    cs_stat = exchange(st.at[2], rc, s_c.at[0], r_c.at[0], pair_peers)
    cs_stat[0].wait()
    m, s = merge([st[2], rc[0]])
    f = jnp.exp(st[0, 0:8, :] - m) / s

    frow = jnp.concatenate([f[i : i + 1, :] for i in range(8)], axis=1)
    part = jnp.dot(split_rows(frow), pb[...], preferred_element_type=F32)
    cm[0] = jnp.sum(part, axis=0, keepdims=True)
    cs = [remote(cm.at[0], cm.at[j], s_m.at[j - 1], r_m.at[j - 1], dp_peers[j - 1]) for j in (1, 2, 3)]
    for c in cs:
        c.start()
    to_cols(acol, f)
    turn(eg2, et2, icol2, first_col + own_cols.astype(F32))
    for c in cs:
        c.wait()
    lr = jnp.log((cm[0] + cm[1] + cm[2] + cm[3]) * classes_over_crops)
    lrow[...] = lr
    lhalf[...] = lrow[:, half_w]

    part = lax.dot_general(split_rows(lr), pb[...], NT, preferred_element_type=F32)
    part = jnp.sum(part, axis=0, keepdims=True)
    for i in range(8):
        qt[0, i : i + 1, :] = part[:, i * 128 : (i + 1) * 128] * f[i : i + 1, :]
    cs = exchange(qt.at[0], qa, s_a.at[1], r_a.at[1], seven_peers)

    for c in cs_stat[1:]:
        c.wait()
    m2, s2 = merge([rc[1], rc[2]])
    to_cols(mcol2, m2)
    to_cols(acol2, 1.0 / s2)
    for i in range(4):
        rows = pl.ds(i * 256, 256)
        pb2[rows, :] = jnp.exp(lb2[rows, :] - mcol2[rows, 0:1]).astype(BF16)
    for c in cs:
        c.wait()
    qt[1] = qt[0] + ((qa[0] + qa[1]) + (qa[2] + qa[3])) + ((qa[4] + qa[5]) + qa[6])
    for c in (cs := exchange(qt.at[1], qb, s_b.at[1], r_b.at[1], beta_peers)):
        c.wait()
    qt[2] = qt[1] + ((qb[0] + qb[1]) + qb[2])
    cs_dot = exchange(qt.at[2], qc, s_c.at[1], r_c.at[1], pair_peers)
    cs_dot[0].wait()
    to_cols(ccol, f * (1.0 - (qt[2] + qc[0])))

    def grad(dst, src, a_ref, c_ref, i_ref, l_ref, width):
        def strip(i, _):
            rows = pl.ds(pl.multiple_of(i * 32, 32), 32)
            a = a_ref[rows, :]
            c = c_ref[rows, :]
            hit = i_ref[rows, :]
            for t in range(width // 128):
                cols = pl.ds(t * 128, 128)
                g = src[rows, cols].astype(F32) * (a * l_ref[:, cols] + c)
                g = jnp.where(hit == t * 128.0, g - 1.0, g)
                dst[rows, cols] = g.astype(BF16)
            return 0

        lax.fori_loop(0, R // 32, strip, 0)

    grad(gb, pb, acol, ccol, icol, lrow, W)

    def half_embed(ci):
        rows = pl.ds(pl.multiple_of(ci * 512, 512), 512)
        v = lax.dot_general(gb[rows, :], w_ref[...], NT, preferred_element_type=F32) * LOGIT_SCALE
        xe[ci] = v.reshape(4, 2, 4, 16, D)

    half_embed(other)
    c1 = remote(xe.at[other], xc, s_x1, r_x1, partner)
    c1.start()

    for c in cs_dot[1:]:
        c.wait()
    to_cols(ccol2, (1.0 - (qc[1] + qc[2])) / s2)
    grad(gb2, pb2, acol2, ccol2, icol2, lhalf, H)

    def outward(t):
        return remote(pp.at[t, pl.ds(0, 3)], pr.at[t], s_po.at[t], r_po.at[t], mate_peer)

    def inward(t):
        return remote(pp.at[t, 0], pr.at[t, 0], s_pi.at[t], r_pi.at[t], mate_peer)

    def proto(t):
        cols = pl.ds(pl.multiple_of(own_cols + t * CW, CW), CW)
        near = pl.ds(t * CW, CW)
        part = jnp.dot(et[...], gb[:, cols], preferred_element_type=F32)
        part = (part + jnp.dot(et2[...], gb2[:, near], preferred_element_type=F32)) * LOGIT_SCALE
        for k in range(4):
            pf[t, k] = part[k * Q : (k + 1) * Q, :]
        pp[t, 0] = pf[t, mate].astype(BF16)

        @pl.when(jnp.logical_not(inner))
        def _():
            pp[t, 1] = pf[t, far_in].astype(BF16)
            pp[t, 2] = pf[t, far_out].astype(BF16)
            outward(t).start()

        @pl.when(inner)
        def _():
            inward(t).start()

    proto(0)
    half_embed(core)
    c1.wait()
    xe[core] = xe[core] + xc[...]
    y1[...] = xe[core].astype(BF16)
    cs = [
        remote(y1.at[add4(beta, k)], xb.at[k - 1], s_x2.at[k - 1], r_x2.at[k - 1], beta_peers[k - 1])
        for k in (1, 2, 3)
    ]
    for c in cs:
        c.start()
    for t in range(1, NC):
        proto(t)

    def relay(t, j):
        peer = (far_in, cls) if j == 0 else (far_out, cls)
        return remote(ps.at[t, j], po2.at[t], s_ps.at[t, j], r_ps.at[t], peer)

    def settle(t):
        @pl.when(inner)
        def _():
            inward(t).wait_send()
            outward(t).wait_recv()
            ps[t, 1] = (pf[t, far_out] + pr[t, 2].astype(F32)).astype(BF16)
            relay(t, 1).start()
            ps[t, 0] = (pf[t, far_in] + pr[t, 1].astype(F32)).astype(BF16)
            relay(t, 0).start()

        @pl.when(jnp.logical_not(inner))
        def _():
            outward(t).wait_send()
            inward(t).wait_recv()

        cols = pl.ds(pl.multiple_of(own_cols + t * CW, CW), CW)
        po_ref[:, cols] = pf[t, dp] + pr[t, 0].astype(F32)

    settle(0)
    for c in cs:
        c.wait()
    own = xe[core, beta] + xb[0].astype(F32) + xb[1].astype(F32) + xb[2].astype(F32)
    xe[core, beta] = own
    y2[...] = own.astype(BF16)
    cs = []
    for j, (dz, da) in enumerate(SEVEN):
        z2, a2 = seven(dz, da)
        cs.append(remote(y2.at[z2, a2], xa.at[j], s_x3.at[j], r_x3.at[j], seven_peers[j]))
    for c in cs:
        c.start()
    for t in range(1, NC):
        settle(t)
    for c in cs:
        c.wait()
    total = xe[core, beta, zh, alpha]
    for j in range(7):
        total = total + xa[j].astype(F32)
    eo_ref[...] = total
    for t in range(NC):
        relay(t, 0).wait_recv()
        cols = pl.ds(pl.multiple_of(H - own_cols + t * CW, CW), CW)
        po_ref[:, cols] = po2[t].astype(F32)

    @pl.when(inner)
    def _():
        for t in range(NC):
            relay(t, 1).wait_send()
            relay(t, 0).wait_send()

    for c in sends:
        c.wait_send()


def on_device(classes_over_crops, embeddings, cluster_ids, prototypes):
    vmem = pl.BlockSpec(memory_space=pltpu.VMEM)
    dma = pltpu.SemaphoreType.DMA
    V = pltpu.VMEM
    scratch = [
        V((D, W), BF16),
        V((2, 4, 2, 4, 16, DX), BF16),
        V((2, 4, 2, 4, 16, DX), BF16),
        V((R, W), BF16),
        V((R, H), F32),
        V((R, H), BF16),
    ] + [V((R, 128), F32)] * 9 + [
        V((D, R), BF16),
        V((D, R), BF16),
        V((R, W), BF16),
        V((R, H), BF16),
        V((3, 16, 128), F32),
        V((7, 16, 128), F32),
        V((3, 16, 128), F32),
        V((3, 16, 128), F32),
        V((4, 1, W), F32),
        V((1, W), F32),
        V((1, H), F32),
        V((3, 8, 128), F32),
        V((7, 8, 128), F32),
        V((3, 8, 128), F32),
        V((3, 8, 128), F32),
        V((NC, 4, Q, CW), F32),
        V((NC, 3, Q, CW), BF16),
        V((NC, 3, Q, CW), BF16),
        V((NC, 2, Q, CW), BF16),
        V((NC, Q, CW), BF16),
        V((2, 4, 2, 4, 16, D), F32),
        V((4, 2, 4, 16, D), F32),
        V((4, 2, 4, 16, D), BF16),
        V((3, 2, 4, 16, D), BF16),
        V((2, 4, 16, D), BF16),
        V((7, 16, D), BF16),
        dma,
        dma((7,)), dma((7,)), dma((3,)), dma((3,)), dma((4,)), dma((4,)), dma, dma, dma((3,)), dma((3,)), dma((4,)), dma((4,)),
        dma((2, 7)), dma((2, 7)), dma((2, 3)), dma((2, 3)), dma((2, 3)), dma((2, 3)),
        dma((3,)), dma((3,)),
        dma((NC,)), dma((NC,)), dma((NC,)), dma((NC,)), dma((NC, 2)), dma((NC,)),
        dma, dma, dma((3,)), dma((3,)), dma((7,)), dma((7,)),
    ]
    return pl.pallas_call(
        functools.partial(kernel, classes_over_crops),
        out_shape=(jax.ShapeDtypeStruct((16, D), F32), jax.ShapeDtypeStruct((Q, W), F32)),
        in_specs=[pl.BlockSpec(memory_space=pltpu.SMEM), vmem, pl.BlockSpec(memory_space=pl.ANY)],
        out_specs=(vmem, vmem),
        scratch_shapes=scratch,
        compiler_params=pltpu.CompilerParams(
            collective_id=0, has_side_effects=True, vmem_limit_bytes=56 * 2**20
        ),
    )(cluster_ids, embeddings, prototypes)


def solution(mesh):
    placed = (P(("dp", "cls"), None), P(("dp", "cls")), P(None, "cls"))
    return jax.shard_map(
        functools.partial(on_device, 131072 / 4096),
        mesh=mesh,
        in_specs=placed,
        out_specs=(P(("dp", "cls"), None), P("dp", "cls")),
        check_vma=False,
    )
```

```python
import functools

import jax
import jax.numpy as jnp
from jax import lax
from jax.experimental import pallas as pl
from jax.experimental.pallas import tpu as pltpu
from jax.sharding import PartitionSpec as P

LOGIT_SCALE = 10.0
MESH = pl.DeviceIdType.MESH
F32 = jnp.float32
BF16 = jnp.bfloat16

D = 384
DX = 512
W = 2048
R = 1024
H = W // 2
NC = 4
CW = H // NC
Q = D // 4
NT = (((1,), (1,)), ((), ()))
SEVEN = [(dz, da) for da in range(4) for dz in range(2) if dz or da]


def split_rows(v):
    hi = v.astype(BF16)
    r1 = v - hi.astype(F32)
    mid = r1.astype(BF16)
    lo = (r1 - mid.astype(F32)).astype(BF16)
    row = lax.broadcasted_iota(jnp.int32, (16, v.shape[1]), 0)
    zero = jnp.zeros((16, v.shape[1]), F32)
    out = jnp.where(row == 0, hi.astype(F32), zero)
    out = jnp.where(row == 1, mid.astype(F32), out)
    out = jnp.where(row == 2, lo.astype(F32), out)
    return out.astype(BF16)


def kernel(classes_over_crops, id_ref, e_ref, w_hbm, eo_ref, po_ref,
           w_ref, eg, eg2, pb, lb2, pb2, mcol, scol, acol, ccol, icol, acol2, ccol2, icol2, mcol2, et, et2, gb, gb2,
           st, ra, rb, rc, cm, lrow, lhalf, qt, qa, qb, qc, pf, pp, pr, pn, rn, ps, po2,
           xe, xc, y1, xb, y2, xa,
           s_w, s_e1, r_e1, s_e2, r_e2, s_e3, r_e3, s_f1, r_f1, s_f2, r_f2, s_f3, r_f3,
           s_a, r_a, s_b, r_b, s_c, r_c, s_m, r_m,
           s_pf, r_pf, s_pn, r_pn, s_ps, r_ps, s_x1, r_x1, s_x2, r_x2, s_x3, r_x3):
    dp = lax.axis_index("dp")
    cls = lax.axis_index("cls")
    core = lax.rem(cls, 2)
    x = lax.rem(cls // 2, 4)
    zh = lax.rem(cls // 8, 2)
    y = cls // 16
    other = 1 - core
    alpha = y * other + x * core
    beta = x * other + y * core
    pair = dp // 2
    mate = dp + 1 - 2 * lax.rem(dp, 2)
    inner = jnp.logical_or(dp == 1, dp == 2)
    far_in = 2 - pair
    far_out = 3 - 3 * pair
    own_cols = pair * H

    def at(zz, aa, bb):
        yy = aa * other + bb * core
        xx = bb * other + aa * core
        return (dp, ((yy * 2 + zz) * 4 + xx) * 2 + core)

    def add4(v, k):
        return lax.rem(v + k, 4)

    def seven(dz, da):
        return lax.rem(zh + dz, 2), add4(alpha, da)

    twin = cls + 1 - 2 * core
    partner = (dp, twin)
    buddy = add4(dp, 2)
    mate_peer = (mate, cls)
    buddy_peer = (buddy, cls)
    dp_peers = [(add4(dp, j), cls) for j in (1, 2, 3)]
    beta_peers = [at(zh, alpha, add4(beta, k)) for k in (1, 2, 3)]
    seven_peers = [at(*seven(dz, da), beta) for dz, da in SEVEN]

    def cross(peer):
        return (dp, peer[1] + 1 - 2 * core)

    wide_peers = [partner] + beta_peers + [cross(p) for p in beta_peers]
    wide_from = [cross(at(zh, add4(alpha, k), beta)) for k in (1, 2, 3)]

    barrier = pltpu.get_barrier_semaphore()
    everyone = [partner] + dp_peers + beta_peers + seven_peers + wide_from
    for peer in everyone:
        pl.semaphore_signal(barrier, inc=1, device_id=peer, device_id_type=MESH)
    load = pltpu.make_async_copy(w_hbm, w_ref, s_w)
    load.start()

    lane = lax.broadcasted_iota(jnp.int32, (16, 128), 1)
    line = lax.broadcasted_iota(jnp.int32, (16, 128), 0)
    ids = jnp.zeros((16, 128), jnp.int32)
    for i in range(16):
        ids = jnp.where(line == i, id_ref[i], ids)
    digits = jnp.where(lane == 0, ids >> 10, jnp.where(lane == 1, (ids >> 5) & 31, jnp.where(lane == 2, ids & 31, 0)))
    eg[core, beta, zh, alpha, :, :D] = e_ref[...]
    eg[core, beta, zh, alpha, :, D:] = digits.astype(F32).astype(BF16)

    pl.semaphore_wait(barrier, len(everyone))

    def remote(src, dst, ssem, rsem, peer):
        return pltpu.make_async_remote_copy(
            src_ref=src, dst_ref=dst, send_sem=ssem, recv_sem=rsem, device_id=peer, device_id_type=MESH
        )

    sends = []

    def post(src, dst, ssem, rsem, peer):
        c = remote(src, dst, ssem, rsem, peer)
        c.start()
        sends.append(c)

    mine = eg.at[core, beta, zh, alpha]
    for j, peer in enumerate(seven_peers):
        post(mine, mine, s_e1.at[j], r_e1.at[j], peer)
    for j, (dz, da) in enumerate(SEVEN):
        block = eg.at[core, beta, lax.rem(zh + dz, 2), add4(alpha, 4 - da)]
        remote(block, block, s_e1.at[j], r_e1.at[j], seven_peers[j]).wait_recv()
    row = eg.at[core, beta]
    for k, peer in enumerate(beta_peers):
        post(row, row, s_e2.at[k], r_e2.at[k], peer)
    post(row, row, s_e3.at[0], r_e3.at[0], partner)
    row2 = eg2.at[core, beta]
    post(row, row2, s_f1, r_f1, buddy_peer)
    load.wait()
    for k in (1, 3, 2):
        b = add4(beta, 4 - k)
        block = eg.at[core, b]
        remote(block, block, s_e2.at[k - 1], r_e2.at[k - 1], beta_peers[k - 1]).wait_recv()
        post(block, block, s_e3.at[k], r_e3.at[k], partner)

    def half_logits(ci):
        for h in range(2):
            left = eg[ci, 2 * h : 2 * h + 2].reshape(256, DX)[:, :D]
            there = pl.ds(pl.multiple_of(ci * (R // 2) + h * 256, 256), 256)
            v = jnp.dot(left, w_ref[...], preferred_element_type=F32) * LOGIT_SCALE
            m = jnp.max(v, axis=1, keepdims=True)
            p = jnp.exp(v - m)
            s = jnp.sum(p, axis=1, keepdims=True)
            pb[there, :] = p.astype(BF16)
            mcol[there, :] = jnp.broadcast_to(m, (256, 128))
            scol[there, :] = jnp.broadcast_to(s, (256, 128))

    half_logits(core)
    for k in (0, 1, 3, 2):
        block = eg.at[other, add4(alpha, 4 - k)]
        remote(block, block, s_e3.at[k], r_e3.at[k], partner).wait_recv()
    half_logits(other)

    remote(row2, row2, s_f1, r_f1, buddy_peer).wait_recv()
    for k, peer in enumerate(beta_peers):
        post(row2, row2, s_f2.at[k], r_f2.at[k], peer)
    post(row2, row2, s_f3.at[0], r_f3.at[0], partner)

    eye = lax.broadcasted_iota(jnp.int32, (128, 128), 0) == lax.broadcasted_iota(jnp.int32, (128, 128), 1)

    def to_line(cols):
        return jnp.sum(jnp.where(eye, cols, 0.0), axis=0, keepdims=True)

    def to_cols(dst, lines):
        for i in range(8):
            dst[i * 128 : (i + 1) * 128, :] = jnp.broadcast_to(lines[i : i + 1, :], (128, 128)).T

    for i in range(8):
        here = pl.ds(i * 128, 128)
        st[0, i : i + 1, :] = to_line(mcol[here, :])
        st[0, 8 + i : 9 + i, :] = to_line(scol[here, :])

    def exchange(src, dst, ssem, rsem, peers):
        cs = [remote(src, dst.at[j], ssem.at[j], rsem.at[j], peer) for j, peer in enumerate(peers)]
        for c in cs:
            c.start()
        return cs

    def merge(parts):
        m = parts[0][0:8, :]
        for v in parts[1:]:
            m = jnp.maximum(m, v[0:8, :])
        s = parts[0][8:16, :] * jnp.exp(parts[0][0:8, :] - m)
        for v in parts[1:]:
            s = s + v[8:16, :] * jnp.exp(v[0:8, :] - m)
        return m, s

    cs = exchange(st.at[0], ra, s_a.at[0], r_a.at[0], seven_peers)

    for k in (1, 3, 2):
        block = eg2.at[core, add4(beta, 4 - k)]
        remote(block, block, s_f2.at[k - 1], r_f2.at[k - 1], beta_peers[k - 1]).wait_recv()
        post(block, block, s_f3.at[k], r_f3.at[k], partner)

    first_col = (cls * W).astype(F32)
    drow = lax.broadcasted_iota(jnp.int32, (128, 128), 0)
    weigh = jnp.where(drow == 0, 1024.0, jnp.where(drow == 1, 32.0, jnp.where(drow == 2, 1.0, 0.0))).astype(BF16)
    ramp = lax.broadcasted_iota(jnp.int32, (1, 128), 1).astype(F32)

    def turn(src, dst_t, dst_i, base):
        rows = src[...].reshape(R, DX)
        for i in range(8):
            dst_t[:, i * 128 : (i + 1) * 128] = rows[i * 128 : (i + 1) * 128, :D].T
        dst_i[...] = jnp.dot(rows[:, D:], weigh, preferred_element_type=F32) - (ramp + base)

    turn(eg, et, icol, first_col)
    for c in cs:
        c.wait()
    m, s = merge([st[0]] + [ra[j] for j in range(7)])
    st[1, 0:8, :] = m
    st[1, 8:16, :] = s
    cs = exchange(st.at[1], rb, s_b.at[0], r_b.at[0], wide_peers)

    for k in (0, 1, 3, 2):
        block = eg2.at[other, add4(alpha, 4 - k)]
        remote(block, block, s_f3.at[k], r_f3.at[k], partner).wait_recv()
    half_w = pl.ds(pl.multiple_of(own_cols, H), H)
    for h in range(2):
        left = eg2[h].reshape(R // 2, DX)[:, :D]
        lb2[h * 512 : (h + 1) * 512, :] = jnp.dot(left, w_ref[:, half_w], preferred_element_type=F32) * LOGIT_SCALE
    for c in cs:
        c.wait()
    m, s = merge([st[1]] + [rb[j] for j in range(7)])
    st[2, 0:8, :] = m
    st[2, 8:16, :] = s
    to_buddy = remote(st.at[2], rc, s_c.at[0], r_c.at[0], buddy_peer)
    to_buddy.start()
    f = jnp.exp(st[0, 0:8, :] - m) / s

    frow = jnp.concatenate([f[i : i + 1, :] for i in range(8)], axis=1)
    part = jnp.dot(split_rows(frow), pb[...], preferred_element_type=F32)
    cm[0] = jnp.sum(part, axis=0, keepdims=True)
    cs = [remote(cm.at[0], cm.at[j], s_m.at[j - 1], r_m.at[j - 1], dp_peers[j - 1]) for j in (1, 2, 3)]
    for c in cs:
        c.start()
    to_cols(acol, f)
    turn(eg2, et2, icol2, first_col + own_cols.astype(F32))
    for c in cs:
        c.wait()
    lr = jnp.log((cm[0] + cm[1] + cm[2] + cm[3]) * classes_over_crops)
    lrow[...] = lr
    lhalf[...] = lrow[:, half_w]

    part = lax.dot_general(split_rows(lr), pb[...], NT, preferred_element_type=F32)
    part = jnp.sum(part, axis=0, keepdims=True)
    for i in range(8):
        qt[0, i : i + 1, :] = part[:, i * 128 : (i + 1) * 128] * f[i : i + 1, :]
    cs = exchange(qt.at[0], qa, s_a.at[1], r_a.at[1], seven_peers)

    to_buddy.wait()
    to_cols(mcol2, rc[0:8, :])
    to_cols(acol2, 1.0 / rc[8:16, :])
    for i in range(4):
        rows = pl.ds(i * 256, 256)
        pb2[rows, :] = jnp.exp(lb2[rows, :] - mcol2[rows, 0:1]).astype(BF16)
    for c in cs:
        c.wait()
    qt[1] = qt[0] + ((qa[0] + qa[1]) + (qa[2] + qa[3])) + ((qa[4] + qa[5]) + qa[6])
    for c in (cs := exchange(qt.at[1], qb, s_b.at[1], r_b.at[1], wide_peers)):
        c.wait()
    qt[2] = qt[1] + ((qb[0] + qb[1]) + (qb[2] + qb[3])) + ((qb[4] + qb[5]) + qb[6])
    to_buddy = remote(qt.at[2], qc, s_c.at[1], r_c.at[1], buddy_peer)
    to_buddy.start()
    to_cols(ccol, f * (1.0 - qt[2]))

    def grad(dst, src, a_ref, c_ref, i_ref, l_ref, first, width):
        def strip(i, _):
            rows = pl.ds(pl.multiple_of(i * 32, 32), 32)
            a = a_ref[rows, :]
            c = c_ref[rows, :]
            hit = i_ref[rows, :]
            for t in range(first // 128, (first + width) // 128):
                cols = pl.ds(t * 128, 128)
                g = src[rows, cols].astype(F32) * (a * l_ref[:, cols] + c)
                g = jnp.where(hit == t * 128.0, g - 1.0, g)
                dst[rows, cols] = g.astype(BF16)
            return 0

        lax.fori_loop(0, R // 32, strip, 0)

    def half_embed(ci):
        rows = pl.ds(pl.multiple_of(ci * 512, 512), 512)
        v = lax.dot_general(gb[rows, :], w_ref[...], NT, preferred_element_type=F32) * LOGIT_SCALE
        xe[ci] = v.reshape(4, 2, 4, 16, D)

    def far(t):
        return remote(pp.at[t], pr.at[t], s_pf.at[t], r_pf.at[t], mate_peer)

    def near(t):
        return remote(pn.at[t], rn.at[t], s_pn.at[t], r_pn.at[t], mate_peer)

    def relay(t, j):
        peer = (far_in, cls) if j == 0 else (far_out, cls)
        return remote(ps.at[t, j], po2.at[t], s_ps.at[t, j], r_ps.at[t], peer)

    def proto(t):
        cols = pl.ds(pl.multiple_of(own_cols + t * CW, CW), CW)
        half = pl.ds(t * CW, CW)
        part = jnp.dot(et[...], gb[:, cols], preferred_element_type=F32)
        part = (part + jnp.dot(et2[...], gb2[:, half], preferred_element_type=F32)) * LOGIT_SCALE
        for k in range(4):
            pf[t, k] = part[k * Q : (k + 1) * Q, :]

        @pl.when(jnp.logical_not(inner))
        def _():
            pp[t, 0] = pf[t, far_in].astype(BF16)
            pp[t, 1] = pf[t, far_out].astype(BF16)
            far(t).start()

        pn[t] = pf[t, mate].astype(BF16)

    def settle_far(t):
        @pl.when(inner)
        def _():
            far(t).wait_recv()
            ps[t, 1] = (pf[t, far_out] + pr[t, 1].astype(F32)).astype(BF16)
            relay(t, 1).start()
            ps[t, 0] = (pf[t, far_in] + pr[t, 0].astype(F32)).astype(BF16)
            relay(t, 0).start()

    grad(gb, pb, acol, ccol, icol, lrow, 0, W)
    to_buddy.wait()
    to_cols(ccol2, (1.0 - qc[...]) / rc[8:16, :])
    grad(gb2, pb2, acol2, ccol2, icol2, lhalf, 0, H // 2)
    proto(0)
    half_embed(other)
    c1 = remote(xe.at[other], xc, s_x1, r_x1, partner)
    c1.start()
    proto(1)
    half_embed(core)
    c1.wait()
    xe[core] = xe[core] + xc[...]
    y1[...] = xe[core].astype(BF16)
    cs = [
        remote(y1.at[add4(beta, k)], xb.at[k - 1], s_x2.at[k - 1], r_x2.at[k - 1], beta_peers[k - 1])
        for k in (1, 2, 3)
    ]
    for c in cs:
        c.start()
    grad(gb2, pb2, acol2, ccol2, icol2, lhalf, H // 2, H // 2)
    proto(2)
    proto(3)
    for t in range(NC):
        near(t).start()
    settle_far(0)
    settle_far(1)
    for c in cs:
        c.wait()
    own = xe[core, beta] + xb[0].astype(F32) + xb[1].astype(F32) + xb[2].astype(F32)
    xe[core, beta] = own
    y2[...] = own.astype(BF16)
    cs = []
    for j, (dz, da) in enumerate(SEVEN):
        z2, a2 = seven(dz, da)
        cs.append(remote(y2.at[z2, a2], xa.at[j], s_x3.at[j], r_x3.at[j], seven_peers[j]))
    for c in cs:
        c.start()
    settle_far(2)
    settle_far(3)
    for t in range(NC):
        near(t).wait()
        cols = pl.ds(pl.multiple_of(own_cols + t * CW, CW), CW)
        po_ref[:, cols] = pf[t, dp] + rn[t].astype(F32)
    for c in cs:
        c.wait()
    total = xe[core, beta, zh, alpha]
    for j in range(7):
        total = total + xa[j].astype(F32)
    eo_ref[...] = total
    for t in range(NC):
        relay(t, 0).wait_recv()
        cols = pl.ds(pl.multiple_of(H - own_cols + t * CW, CW), CW)
        po_ref[:, cols] = po2[t].astype(F32)

    @pl.when(inner)
    def _():
        for t in range(NC):
            relay(t, 1).wait_send()
            relay(t, 0).wait_send()

    @pl.when(jnp.logical_not(inner))
    def _():
        for t in range(NC):
            far(t).wait_send()

    for c in sends:
        c.wait_send()


def on_device(classes_over_crops, embeddings, cluster_ids, prototypes):
    vmem = pl.BlockSpec(memory_space=pltpu.VMEM)
    dma = pltpu.SemaphoreType.DMA
    V = pltpu.VMEM
    scratch = [
        V((D, W), BF16),
        V((2, 4, 2, 4, 16, DX), BF16),
        V((2, 4, 2, 4, 16, DX), BF16),
        V((R, W), BF16),
        V((R, H), F32),
        V((R, H), BF16),
    ] + [V((R, 128), F32)] * 9 + [
        V((D, R), BF16),
        V((D, R), BF16),
        V((R, W), BF16),
        V((R, H), BF16),
        V((3, 16, 128), F32),
        V((7, 16, 128), F32),
        V((7, 16, 128), F32),
        V((16, 128), F32),
        V((4, 1, W), F32),
        V((1, W), F32),
        V((1, H), F32),
        V((3, 8, 128), F32),
        V((7, 8, 128), F32),
        V((7, 8, 128), F32),
        V((8, 128), F32),
        V((NC, 4, Q, CW), F32),
        V((NC, 2, Q, CW), BF16),
        V((NC, 2, Q, CW), BF16),
        V((NC, Q, CW), BF16),
        V((NC, Q, CW), BF16),
        V((NC, 2, Q, CW), BF16),
        V((NC, Q, CW), BF16),
        V((2, 4, 2, 4, 16, D), F32),
        V((4, 2, 4, 16, D), F32),
        V((4, 2, 4, 16, D), BF16),
        V((3, 2, 4, 16, D), BF16),
        V((2, 4, 16, D), BF16),
        V((7, 16, D), BF16),
        dma,
        dma((7,)), dma((7,)), dma((3,)), dma((3,)), dma((4,)), dma((4,)), dma, dma, dma((3,)), dma((3,)), dma((4,)), dma((4,)),
        dma((2, 7)), dma((2, 7)), dma((2, 7)), dma((2, 7)), dma((2,)), dma((2,)),
        dma((3,)), dma((3,)),
        dma((NC,)), dma((NC,)), dma((NC,)), dma((NC,)), dma((NC, 2)), dma((NC,)),
        dma, dma, dma((3,)), dma((3,)), dma((7,)), dma((7,)),
    ]
    halves = pl.pallas_call(
        functools.partial(kernel, classes_over_crops),
        out_shape=(jax.ShapeDtypeStruct((16, D), F32), jax.ShapeDtypeStruct((Q, W), F32)),
        in_specs=[pl.BlockSpec(memory_space=pltpu.SMEM), vmem, pl.BlockSpec(memory_space=pl.ANY)],
        out_specs=(vmem, vmem),
        scratch_shapes=scratch,
        compiler_params=pltpu.CompilerParams(
            collective_id=0, has_side_effects=True, vmem_limit_bytes=56 * 2**20
        ),
    )(cluster_ids, embeddings, prototypes)

    any_space = pl.BlockSpec(memory_space=pl.ANY)

    def hand_over(a_ref, b_ref, a_out, b_out, sems):
        a_out[...] = a_ref[...]
        b_out[...] = b_ref[...]

    return pl.pallas_call(
        hand_over,
        out_shape=(jax.ShapeDtypeStruct((16, D), F32), jax.ShapeDtypeStruct((Q, W), F32)),
        in_specs=[vmem] * 2,
        out_specs=(vmem,) * 2,
        scratch_shapes=[dma((2,))],
    )(*halves)


def solution(mesh):
    placed = (P(("dp", "cls"), None), P(("dp", "cls")), P(None, "cls"))
    return jax.shard_map(
        functools.partial(on_device, 131072 / 4096),
        mesh=mesh,
        in_specs=placed,
        out_specs=(P(("dp", "cls"), None), P("dp", "cls")),
        check_vma=False,
    )
```

```python
import functools

import jax
import jax.numpy as jnp
from jax import lax
from jax.experimental import pallas as pl
from jax.experimental.pallas import tpu as pltpu
from jax.sharding import PartitionSpec as P

LOGIT_SCALE = 10.0
MESH = pl.DeviceIdType.MESH
F32 = jnp.float32
BF16 = jnp.bfloat16

D = 384
DX = 512
W = 2048
R = 1024
H = W // 2
NC = 4
CW = H // NC
Q = D // 4
NT = (((1,), (1,)), ((), ()))
SEVEN = [(dz, da) for da in range(4) for dz in range(2) if dz or da]


def split_rows(v):
    hi = v.astype(BF16)
    r1 = v - hi.astype(F32)
    mid = r1.astype(BF16)
    lo = (r1 - mid.astype(F32)).astype(BF16)
    row = lax.broadcasted_iota(jnp.int32, (16, v.shape[1]), 0)
    zero = jnp.zeros((16, v.shape[1]), F32)
    out = jnp.where(row == 0, hi.astype(F32), zero)
    out = jnp.where(row == 1, mid.astype(F32), out)
    out = jnp.where(row == 2, lo.astype(F32), out)
    return out.astype(BF16)


def kernel(classes_over_crops, id_ref, e_ref, w_hbm, eo_ref, po_ref,
           w_ref, eg, eg2, pb, lb2, pb2, mcol, scol, acol, ccol, icol, acol2, ccol2, icol2, mcol2, et, et2, gb, gb2,
           st, ra, rb, rc, cm, lrow, lhalf, qt, qa, qb, qc, pf, pp, pr, pn, rn, ps, po2,
           xe, xc, y1, xb, y2, xa,
           s_w, s_e1, r_e1, s_e2, r_e2, s_e3, r_e3, s_f1, r_f1, s_f2, r_f2, s_f3, r_f3,
           s_a, r_a, s_b, r_b, s_c, r_c, s_m, r_m,
           s_pf, r_pf, s_pn, r_pn, s_ps, r_ps, s_x1, r_x1, s_x2, r_x2, s_x3, r_x3):
    dp = lax.axis_index("dp")
    cls = lax.axis_index("cls")
    core = lax.rem(cls, 2)
    x = lax.rem(cls // 2, 4)
    zh = lax.rem(cls // 8, 2)
    y = cls // 16
    other = 1 - core
    alpha = y * other + x * core
    beta = x * other + y * core
    pair = dp // 2
    mate = dp + 1 - 2 * lax.rem(dp, 2)
    inner = jnp.logical_or(dp == 1, dp == 2)
    far_in = 2 - pair
    far_out = 3 - 3 * pair
    own_cols = pair * H

    def at(zz, aa, bb):
        yy = aa * other + bb * core
        xx = bb * other + aa * core
        return (dp, ((yy * 2 + zz) * 4 + xx) * 2 + core)

    def add4(v, k):
        return lax.rem(v + k, 4)

    def seven(dz, da):
        return lax.rem(zh + dz, 2), add4(alpha, da)

    twin = cls + 1 - 2 * core
    partner = (dp, twin)
    buddy = add4(dp, 2)
    mate_peer = (mate, cls)
    buddy_peer = (buddy, cls)
    dp_peers = [(add4(dp, j), cls) for j in (1, 2, 3)]
    beta_peers = [at(zh, alpha, add4(beta, k)) for k in (1, 2, 3)]
    seven_peers = [at(*seven(dz, da), beta) for dz, da in SEVEN]

    def cross(peer):
        return (dp, peer[1] + 1 - 2 * core)

    wide_peers = [partner] + beta_peers + [cross(p) for p in beta_peers]
    wide_from = [cross(at(zh, add4(alpha, k), beta)) for k in (1, 2, 3)]

    barrier = pltpu.get_barrier_semaphore()
    everyone = [partner] + dp_peers + beta_peers + seven_peers + wide_from
    for peer in everyone:
        pl.semaphore_signal(barrier, inc=1, device_id=peer, device_id_type=MESH)
    load = pltpu.make_async_copy(w_hbm, w_ref, s_w)
    load.start()

    lane = lax.broadcasted_iota(jnp.int32, (16, 128), 1)
    line = lax.broadcasted_iota(jnp.int32, (16, 128), 0)
    ids = jnp.zeros((16, 128), jnp.int32)
    for i in range(16):
        ids = jnp.where(line == i, id_ref[i], ids)
    digits = jnp.where(lane == 0, ids >> 10, jnp.where(lane == 1, (ids >> 5) & 31, jnp.where(lane == 2, ids & 31, 0)))
    eg[core, beta, zh, alpha, :, :D] = e_ref[...]
    eg[core, beta, zh, alpha, :, D:] = digits.astype(F32).astype(BF16)

    pl.semaphore_wait(barrier, len(everyone))

    def remote(src, dst, ssem, rsem, peer):
        return pltpu.make_async_remote_copy(
            src_ref=src, dst_ref=dst, send_sem=ssem, recv_sem=rsem, device_id=peer, device_id_type=MESH
        )

    sends = []

    def post(src, dst, ssem, rsem, peer):
        c = remote(src, dst, ssem, rsem, peer)
        c.start()
        sends.append(c)

    mine = eg.at[core, beta, zh, alpha]
    for j, peer in enumerate(seven_peers):
        post(mine, mine, s_e1.at[j], r_e1.at[j], peer)
    for j, (dz, da) in enumerate(SEVEN):
        block = eg.at[core, beta, lax.rem(zh + dz, 2), add4(alpha, 4 - da)]
        remote(block, block, s_e1.at[j], r_e1.at[j], seven_peers[j]).wait_recv()
    row = eg.at[core, beta]
    for k, peer in enumerate(beta_peers):
        post(row, row, s_e2.at[k], r_e2.at[k], peer)
    post(row, row, s_e3.at[0], r_e3.at[0], partner)
    row2 = eg2.at[core, beta]
    post(row, row2, s_f1, r_f1, buddy_peer)
    load.wait()
    for k in (1, 3, 2):
        b = add4(beta, 4 - k)
        block = eg.at[core, b]
        remote(block, block, s_e2.at[k - 1], r_e2.at[k - 1], beta_peers[k - 1]).wait_recv()
        post(block, block, s_e3.at[k], r_e3.at[k], partner)

    def half_logits(ci):
        for h in range(2):
            left = eg[ci, 2 * h : 2 * h + 2].reshape(256, DX)[:, :D]
            there = pl.ds(pl.multiple_of(ci * (R // 2) + h * 256, 256), 256)
            v = jnp.dot(left, w_ref[...], preferred_element_type=F32) * LOGIT_SCALE
            m = jnp.max(v, axis=1, keepdims=True)
            p = jnp.exp(v - m)
            s = jnp.sum(p, axis=1, keepdims=True)
            pb[there, :] = p.astype(BF16)
            mcol[there, :] = jnp.broadcast_to(m, (256, 128))
            scol[there, :] = jnp.broadcast_to(s, (256, 128))

    half_logits(core)
    for k in (0, 1, 3, 2):
        block = eg.at[other, add4(alpha, 4 - k)]
        remote(block, block, s_e3.at[k], r_e3.at[k], partner).wait_recv()
    half_logits(other)

    remote(row2, row2, s_f1, r_f1, buddy_peer).wait_recv()
    for k, peer in enumerate(beta_peers):
        post(row2, row2, s_f2.at[k], r_f2.at[k], peer)
    post(row2, row2, s_f3.at[0], r_f3.at[0], partner)

    eye = lax.broadcasted_iota(jnp.int32, (128, 128), 0) == lax.broadcasted_iota(jnp.int32, (128, 128), 1)

    def to_line(cols):
        return jnp.sum(jnp.where(eye, cols, 0.0), axis=0, keepdims=True)

    def to_cols(dst, lines):
        for i in range(8):
            dst[i * 128 : (i + 1) * 128, :] = jnp.broadcast_to(lines[i : i + 1, :], (128, 128)).T

    for i in range(8):
        here = pl.ds(i * 128, 128)
        st[0, i : i + 1, :] = to_line(mcol[here, :])
        st[0, 8 + i : 9 + i, :] = to_line(scol[here, :])

    def exchange(src, dst, ssem, rsem, peers):
        cs = [remote(src, dst.at[j], ssem.at[j], rsem.at[j], peer) for j, peer in enumerate(peers)]
        for c in cs:
            c.start()
        return cs

    def merge(parts):
        m = parts[0][0:8, :]
        for v in parts[1:]:
            m = jnp.maximum(m, v[0:8, :])
        s = parts[0][8:16, :] * jnp.exp(parts[0][0:8, :] - m)
        for v in parts[1:]:
            s = s + v[8:16, :] * jnp.exp(v[0:8, :] - m)
        return m, s

    cs = exchange(st.at[0], ra, s_a.at[0], r_a.at[0], seven_peers)

    for k in (1, 3, 2):
        block = eg2.at[core, add4(beta, 4 - k)]
        remote(block, block, s_f2.at[k - 1], r_f2.at[k - 1], beta_peers[k - 1]).wait_recv()
        post(block, block, s_f3.at[k], r_f3.at[k], partner)

    first_col = (cls * W).astype(F32)
    drow = lax.broadcasted_iota(jnp.int32, (128, 128), 0)
    weigh = jnp.where(drow == 0, 1024.0, jnp.where(drow == 1, 32.0, jnp.where(drow == 2, 1.0, 0.0))).astype(BF16)
    ramp = lax.broadcasted_iota(jnp.int32, (1, 128), 1).astype(F32)

    def turn(src, dst_t, dst_i, base):
        rows = src[...].reshape(R, DX)
        for i in range(8):
            dst_t[:, i * 128 : (i + 1) * 128] = rows[i * 128 : (i + 1) * 128, :D].T
        dst_i[...] = jnp.dot(rows[:, D:], weigh, preferred_element_type=F32) - (ramp + base)

    turn(eg, et, icol, first_col)
    for c in cs:
        c.wait()
    m, s = merge([st[0]] + [ra[j] for j in range(7)])
    st[1, 0:8, :] = m
    st[1, 8:16, :] = s
    cs = exchange(st.at[1], rb, s_b.at[0], r_b.at[0], wide_peers)

    for k in (0, 1, 3, 2):
        block = eg2.at[other, add4(alpha, 4 - k)]
        remote(block, block, s_f3.at[k], r_f3.at[k], partner).wait_recv()
    half_w = pl.ds(pl.multiple_of(own_cols, H), H)
    for h in range(2):
        left = eg2[h].reshape(R // 2, DX)[:, :D]
        lb2[h * 512 : (h + 1) * 512, :] = jnp.dot(left, w_ref[:, half_w], preferred_element_type=F32) * LOGIT_SCALE
    for c in cs:
        c.wait()
    m, s = merge([st[1]] + [rb[j] for j in range(7)])
    st[2, 0:8, :] = m
    st[2, 8:16, :] = s
    to_buddy = remote(st.at[2], rc, s_c.at[0], r_c.at[0], buddy_peer)
    to_buddy.start()
    f = jnp.exp(st[0, 0:8, :] - m) / s

    frow = jnp.concatenate([f[i : i + 1, :] for i in range(8)], axis=1)
    part = jnp.dot(split_rows(frow), pb[...], preferred_element_type=F32)
    cm[0] = jnp.sum(part, axis=0, keepdims=True)
    cs = [remote(cm.at[0], cm.at[j], s_m.at[j - 1], r_m.at[j - 1], dp_peers[j - 1]) for j in (1, 2, 3)]
    for c in cs:
        c.start()
    to_cols(acol, f)
    turn(eg2, et2, icol2, first_col + own_cols.astype(F32))
    for c in cs:
        c.wait()
    lr = jnp.log((cm[0] + cm[1] + cm[2] + cm[3]) * classes_over_crops)
    lrow[...] = lr
    lhalf[...] = lrow[:, half_w]

    part = lax.dot_general(split_rows(lr), pb[...], NT, preferred_element_type=F32)
    part = jnp.sum(part, axis=0, keepdims=True)
    for i in range(8):
        qt[0, i : i + 1, :] = part[:, i * 128 : (i + 1) * 128] * f[i : i + 1, :]
    cs = exchange(qt.at[0], qa, s_a.at[1], r_a.at[1], seven_peers)

    to_buddy.wait()
    to_cols(mcol2, rc[0:8, :])
    to_cols(acol2, 1.0 / rc[8:16, :])
    for i in range(4):
        rows = pl.ds(i * 256, 256)
        pb2[rows, :] = jnp.exp(lb2[rows, :] - mcol2[rows, 0:1]).astype(BF16)
    for c in cs:
        c.wait()
    qt[1] = qt[0] + ((qa[0] + qa[1]) + (qa[2] + qa[3])) + ((qa[4] + qa[5]) + qa[6])
    for c in (cs := exchange(qt.at[1], qb, s_b.at[1], r_b.at[1], wide_peers)):
        c.wait()
    qt[2] = qt[1] + ((qb[0] + qb[1]) + (qb[2] + qb[3])) + ((qb[4] + qb[5]) + qb[6])
    to_buddy = remote(qt.at[2], qc, s_c.at[1], r_c.at[1], buddy_peer)
    to_buddy.start()
    to_cols(ccol, f * (1.0 - qt[2]))

    def grad(dst, src, a_ref, c_ref, i_ref, l_ref, first, width):
        def strip(i, _):
            rows = pl.ds(pl.multiple_of(i * 32, 32), 32)
            a = a_ref[rows, :]
            c = c_ref[rows, :]
            hit = i_ref[rows, :]
            for t in range(first // 128, (first + width) // 128):
                cols = pl.ds(t * 128, 128)
                g = src[rows, cols].astype(F32) * (a * l_ref[:, cols] + c)
                g = jnp.where(hit == t * 128.0, g - 1.0, g)
                dst[rows, cols] = g.astype(BF16)
            return 0

        lax.fori_loop(0, R // 32, strip, 0)

    def half_embed(ci):
        rows = pl.ds(pl.multiple_of(ci * 512, 512), 512)
        v = lax.dot_general(gb[rows, :], w_ref[...], NT, preferred_element_type=F32) * LOGIT_SCALE
        xe[ci] = v.reshape(4, 2, 4, 16, D)

    def far(t):
        return remote(pp.at[t], pr.at[t], s_pf.at[t], r_pf.at[t], mate_peer)

    def near(t):
        return remote(pn.at[t], rn.at[t], s_pn.at[t], r_pn.at[t], mate_peer)

    def relay(t, j):
        peer = (far_in, cls) if j == 0 else (far_out, cls)
        return remote(ps.at[t, j], po2.at[t], s_ps.at[t, j], r_ps.at[t], peer)

    def proto(t):
        cols = pl.ds(pl.multiple_of(own_cols + t * CW, CW), CW)
        half = pl.ds(t * CW, CW)
        part = jnp.dot(et[...], gb[:, cols], preferred_element_type=F32)
        part = (part + jnp.dot(et2[...], gb2[:, half], preferred_element_type=F32)) * LOGIT_SCALE
        for k in range(4):
            pf[t, k] = part[k * Q : (k + 1) * Q, :]

        @pl.when(jnp.logical_not(inner))
        def _():
            pp[t, 0] = pf[t, far_in].astype(BF16)
            pp[t, 1] = pf[t, far_out].astype(BF16)
            far(t).start()

        pn[t] = pf[t, mate].astype(BF16)
        near(t).start()

    def settle_far(t):
        @pl.when(inner)
        def _():
            far(t).wait_recv()
            ps[t, 1] = (pf[t, far_out] + pr[t, 1].astype(F32)).astype(BF16)
            relay(t, 1).start()
            ps[t, 0] = (pf[t, far_in] + pr[t, 0].astype(F32)).astype(BF16)
            relay(t, 0).start()

    grad(gb, pb, acol, ccol, icol, lrow, 0, W)
    to_buddy.wait()
    to_cols(ccol2, (1.0 - qc[...]) / rc[8:16, :])
    grad(gb2, pb2, acol2, ccol2, icol2, lhalf, 0, H // 2)
    proto(0)
    proto(1)
    half_embed(other)
    c1 = remote(xe.at[other], xc, s_x1, r_x1, partner)
    c1.start()
    grad(gb2, pb2, acol2, ccol2, icol2, lhalf, H // 2, H // 2)
    proto(2)
    proto(3)
    half_embed(core)
    c1.wait()
    xe[core] = xe[core] + xc[...]
    y1[...] = xe[core].astype(BF16)
    cs = [
        remote(y1.at[add4(beta, k)], xb.at[k - 1], s_x2.at[k - 1], r_x2.at[k - 1], beta_peers[k - 1])
        for k in (1, 2, 3)
    ]
    for c in cs:
        c.start()
    settle_far(0)
    settle_far(1)
    for c in cs:
        c.wait()
    own = xe[core, beta] + xb[0].astype(F32) + xb[1].astype(F32) + xb[2].astype(F32)
    xe[core, beta] = own
    y2[...] = own.astype(BF16)
    cs = []
    for j, (dz, da) in enumerate(SEVEN):
        z2, a2 = seven(dz, da)
        cs.append(remote(y2.at[z2, a2], xa.at[j], s_x3.at[j], r_x3.at[j], seven_peers[j]))
    for c in cs:
        c.start()
    settle_far(2)
    settle_far(3)
    for t in range(NC):
        near(t).wait()
        cols = pl.ds(pl.multiple_of(own_cols + t * CW, CW), CW)
        po_ref[:, cols] = pf[t, dp] + rn[t].astype(F32)
    for c in cs:
        c.wait()
    total = xe[core, beta, zh, alpha]
    for j in range(7):
        total = total + xa[j].astype(F32)
    eo_ref[...] = total
    for t in range(NC):
        relay(t, 0).wait_recv()
        cols = pl.ds(pl.multiple_of(H - own_cols + t * CW, CW), CW)
        po_ref[:, cols] = po2[t].astype(F32)

    @pl.when(inner)
    def _():
        for t in range(NC):
            relay(t, 1).wait_send()
            relay(t, 0).wait_send()

    @pl.when(jnp.logical_not(inner))
    def _():
        for t in range(NC):
            far(t).wait_send()

    for c in sends:
        c.wait_send()


def on_device(classes_over_crops, embeddings, cluster_ids, prototypes):
    vmem = pl.BlockSpec(memory_space=pltpu.VMEM)
    dma = pltpu.SemaphoreType.DMA
    V = pltpu.VMEM
    scratch = [
        V((D, W), BF16),
        V((2, 4, 2, 4, 16, DX), BF16),
        V((2, 4, 2, 4, 16, DX), BF16),
        V((R, W), BF16),
        V((R, H), F32),
        V((R, H), BF16),
    ] + [V((R, 128), F32)] * 9 + [
        V((D, R), BF16),
        V((D, R), BF16),
        V((R, W), BF16),
        V((R, H), BF16),
        V((3, 16, 128), F32),
        V((7, 16, 128), F32),
        V((7, 16, 128), F32),
        V((16, 128), F32),
        V((4, 1, W), F32),
        V((1, W), F32),
        V((1, H), F32),
        V((3, 8, 128), F32),
        V((7, 8, 128), F32),
        V((7, 8, 128), F32),
        V((8, 128), F32),
        V((NC, 4, Q, CW), F32),
        V((NC, 2, Q, CW), BF16),
        V((NC, 2, Q, CW), BF16),
        V((NC, Q, CW), BF16),
        V((NC, Q, CW), BF16),
        V((NC, 2, Q, CW), BF16),
        V((NC, Q, CW), BF16),
        V((2, 4, 2, 4, 16, D), F32),
        V((4, 2, 4, 16, D), F32),
        V((4, 2, 4, 16, D), BF16),
        V((3, 2, 4, 16, D), BF16),
        V((2, 4, 16, D), BF16),
        V((7, 16, D), BF16),
        dma,
        dma((7,)), dma((7,)), dma((3,)), dma((3,)), dma((4,)), dma((4,)), dma, dma, dma((3,)), dma((3,)), dma((4,)), dma((4,)),
        dma((2, 7)), dma((2, 7)), dma((2, 7)), dma((2, 7)), dma((2,)), dma((2,)),
        dma((3,)), dma((3,)),
        dma((NC,)), dma((NC,)), dma((NC,)), dma((NC,)), dma((NC, 2)), dma((NC,)),
        dma, dma, dma((3,)), dma((3,)), dma((7,)), dma((7,)),
    ]
    halves = pl.pallas_call(
        functools.partial(kernel, classes_over_crops),
        out_shape=(jax.ShapeDtypeStruct((16, D), F32), jax.ShapeDtypeStruct((Q, W), F32)),
        in_specs=[pl.BlockSpec(memory_space=pltpu.SMEM), vmem, pl.BlockSpec(memory_space=pl.ANY)],
        out_specs=(vmem, vmem),
        scratch_shapes=scratch,
        compiler_params=pltpu.CompilerParams(
            collective_id=0, has_side_effects=True, vmem_limit_bytes=56 * 2**20
        ),
    )(cluster_ids, embeddings, prototypes)

    any_space = pl.BlockSpec(memory_space=pl.ANY)

    def hand_over(a_ref, b_ref, a_out, b_out, sems):
        a_out[...] = a_ref[...]
        b_out[...] = b_ref[...]

    return pl.pallas_call(
        hand_over,
        out_shape=(jax.ShapeDtypeStruct((16, D), F32), jax.ShapeDtypeStruct((Q, W), F32)),
        in_specs=[vmem] * 2,
        out_specs=(vmem,) * 2,
        scratch_shapes=[dma((2,))],
    )(*halves)


def solution(mesh):
    placed = (P(("dp", "cls"), None), P(("dp", "cls")), P(None, "cls"))
    return jax.shard_map(
        functools.partial(on_device, 131072 / 4096),
        mesh=mesh,
        in_specs=placed,
        out_specs=(P(("dp", "cls"), None), P("dp", "cls")),
        check_vma=False,
    )
```

```python
import functools

import jax
import jax.numpy as jnp
from jax import lax
from jax.experimental import pallas as pl
from jax.experimental.pallas import tpu as pltpu
from jax.sharding import PartitionSpec as P

LOGIT_SCALE = 10.0
MESH = pl.DeviceIdType.MESH
F32 = jnp.float32
BF16 = jnp.bfloat16

D = 384
DX = 512
W = 2048
R = 1024
H = W // 2
NC = 4
CW = H // NC
Q = D // 4
NT = (((1,), (1,)), ((), ()))
SEVEN = [(1, 2), (1, 1), (1, 3), (1, 0), (0, 2), (0, 1), (0, 3)]


def split_rows(v):
    hi = v.astype(BF16)
    r1 = v - hi.astype(F32)
    mid = r1.astype(BF16)
    lo = (r1 - mid.astype(F32)).astype(BF16)
    row = lax.broadcasted_iota(jnp.int32, (16, v.shape[1]), 0)
    zero = jnp.zeros((16, v.shape[1]), F32)
    out = jnp.where(row == 0, hi.astype(F32), zero)
    out = jnp.where(row == 1, mid.astype(F32), out)
    out = jnp.where(row == 2, lo.astype(F32), out)
    return out.astype(BF16)


def kernel(classes_over_crops, id_ref, e_ref, w_hbm, eo_ref, po_ref,
           w_ref, eg, eg2, pb, lb2, pb2, mcol, scol, acol, ccol, icol, acol2, ccol2, icol2, mcol2, et, et2, gb, gb2,
           st, ra, rb, rc, cm, lrow, lhalf, qt, qa, qb, qc, pf, pp, pr, pn, rn, ps, po2,
           xe, xc, y1, xb, y2, xa,
           s_w, s_e1, r_e1, s_e2, r_e2, s_e3, r_e3, s_f1, r_f1, s_f2, r_f2, s_f3, r_f3,
           s_a, r_a, s_b, r_b, s_c, r_c, s_m, r_m,
           s_pf, r_pf, s_pn, r_pn, s_ps, r_ps, s_x1, r_x1, s_x2, r_x2, s_x3, r_x3):
    dp = lax.axis_index("dp")
    cls = lax.axis_index("cls")
    core = lax.rem(cls, 2)
    x = lax.rem(cls // 2, 4)
    zh = lax.rem(cls // 8, 2)
    y = cls // 16
    other = 1 - core
    alpha = y * other + x * core
    beta = x * other + y * core
    pair = dp // 2
    mate = dp + 1 - 2 * lax.rem(dp, 2)
    inner = jnp.logical_or(dp == 1, dp == 2)
    far_in = 2 - pair
    far_out = 3 - 3 * pair
    own_cols = pair * H

    def at(zz, aa, bb):
        yy = aa * other + bb * core
        xx = bb * other + aa * core
        return (dp, ((yy * 2 + zz) * 4 + xx) * 2 + core)

    def add4(v, k):
        return lax.rem(v + k, 4)

    def seven(dz, da):
        return lax.rem(zh + dz, 2), add4(alpha, da)

    twin = cls + 1 - 2 * core
    partner = (dp, twin)
    buddy = add4(dp, 2)
    mate_peer = (mate, cls)
    buddy_peer = (buddy, cls)
    dp_peers = [(add4(dp, j), cls) for j in (1, 2, 3)]
    beta_peers = [at(zh, alpha, add4(beta, k)) for k in (1, 2, 3)]
    seven_peers = [at(*seven(dz, da), beta) for dz, da in SEVEN]

    def cross(peer):
        return (dp, peer[1] + 1 - 2 * core)

    wide_peers = [cross(beta_peers[1]), beta_peers[1], cross(beta_peers[0]), cross(beta_peers[2])]
    wide_peers = wide_peers + [beta_peers[0], beta_peers[2], partner]
    wide_from = [cross(at(zh, add4(alpha, k), beta)) for k in (1, 2, 3)]

    barrier = pltpu.get_barrier_semaphore()
    everyone = seven_peers + dp_peers + wide_from + beta_peers + [partner]
    for peer in everyone:
        pl.semaphore_signal(barrier, inc=1, device_id=peer, device_id_type=MESH)
    load = pltpu.make_async_copy(w_hbm, w_ref, s_w)
    load.start()

    lane = lax.broadcasted_iota(jnp.int32, (16, 128), 1)
    line = lax.broadcasted_iota(jnp.int32, (16, 128), 0)
    ids = jnp.zeros((16, 128), jnp.int32)
    for i in range(16):
        ids = jnp.where(line == i, id_ref[i], ids)
    digits = jnp.where(lane == 0, ids >> 10, jnp.where(lane == 1, (ids >> 5) & 31, jnp.where(lane == 2, ids & 31, 0)))
    eg[core, beta, zh, alpha, :, :D] = e_ref[...]
    eg[core, beta, zh, alpha, :, D:] = digits.astype(F32).astype(BF16)

    pl.semaphore_wait(barrier, len(everyone))

    def remote(src, dst, ssem, rsem, peer):
        return pltpu.make_async_remote_copy(
            src_ref=src, dst_ref=dst, send_sem=ssem, recv_sem=rsem, device_id=peer, device_id_type=MESH
        )

    sends = []

    def post(src, dst, ssem, rsem, peer):
        c = remote(src, dst, ssem, rsem, peer)
        c.start()
        sends.append(c)

    mine = eg.at[core, beta, zh, alpha]
    for j, peer in enumerate(seven_peers):
        post(mine, mine, s_e1.at[j], r_e1.at[j], peer)
    for j, (dz, da) in enumerate(SEVEN):
        block = eg.at[core, beta, lax.rem(zh + dz, 2), add4(alpha, 4 - da)]
        remote(block, block, s_e1.at[j], r_e1.at[j], seven_peers[j]).wait_recv()
    row = eg.at[core, beta]
    for k, peer in enumerate(beta_peers):
        post(row, row, s_e2.at[k], r_e2.at[k], peer)
    post(row, row, s_e3.at[0], r_e3.at[0], partner)
    row2 = eg2.at[core, beta]
    post(row, row2, s_f1, r_f1, buddy_peer)
    load.wait()
    for k in (1, 3, 2):
        b = add4(beta, 4 - k)
        block = eg.at[core, b]
        remote(block, block, s_e2.at[k - 1], r_e2.at[k - 1], beta_peers[k - 1]).wait_recv()
        post(block, block, s_e3.at[k], r_e3.at[k], partner)

    def half_logits(ci):
        for h in range(2):
            left = eg[ci, 2 * h : 2 * h + 2].reshape(256, DX)[:, :D]
            there = pl.ds(pl.multiple_of(ci * (R // 2) + h * 256, 256), 256)
            v = jnp.dot(left, w_ref[...], preferred_element_type=F32) * LOGIT_SCALE
            m = jnp.max(v, axis=1, keepdims=True)
            p = jnp.exp(v - m)
            s = jnp.sum(p, axis=1, keepdims=True)
            pb[there, :] = p.astype(BF16)
            mcol[there, :] = jnp.broadcast_to(m, (256, 128))
            scol[there, :] = jnp.broadcast_to(s, (256, 128))

    half_logits(core)
    for k in (0, 1, 3, 2):
        block = eg.at[other, add4(alpha, 4 - k)]
        remote(block, block, s_e3.at[k], r_e3.at[k], partner).wait_recv()
    half_logits(other)

    remote(row2, row2, s_f1, r_f1, buddy_peer).wait_recv()
    for k, peer in enumerate(beta_peers):
        post(row2, row2, s_f2.at[k], r_f2.at[k], peer)
    post(row2, row2, s_f3.at[0], r_f3.at[0], partner)

    eye = lax.broadcasted_iota(jnp.int32, (128, 128), 0) == lax.broadcasted_iota(jnp.int32, (128, 128), 1)

    def to_line(cols):
        return jnp.sum(jnp.where(eye, cols, 0.0), axis=0, keepdims=True)

    def to_cols(dst, lines):
        for i in range(8):
            dst[i * 128 : (i + 1) * 128, :] = jnp.broadcast_to(lines[i : i + 1, :], (128, 128)).T

    for i in range(8):
        here = pl.ds(i * 128, 128)
        st[0, i : i + 1, :] = to_line(mcol[here, :])
        st[0, 8 + i : 9 + i, :] = to_line(scol[here, :])

    def exchange(src, dst, ssem, rsem, peers):
        cs = [remote(src, dst.at[j], ssem.at[j], rsem.at[j], peer) for j, peer in enumerate(peers)]
        for c in cs:
            c.start()
        return cs

    def merge(parts):
        m = parts[0][0:8, :]
        for v in parts[1:]:
            m = jnp.maximum(m, v[0:8, :])
        s = parts[0][8:16, :] * jnp.exp(parts[0][0:8, :] - m)
        for v in parts[1:]:
            s = s + v[8:16, :] * jnp.exp(v[0:8, :] - m)
        return m, s

    cs = exchange(st.at[0], ra, s_a.at[0], r_a.at[0], seven_peers)

    for k in (1, 3, 2):
        block = eg2.at[core, add4(beta, 4 - k)]
        remote(block, block, s_f2.at[k - 1], r_f2.at[k - 1], beta_peers[k - 1]).wait_recv()
        post(block, block, s_f3.at[k], r_f3.at[k], partner)

    first_col = (cls * W).astype(F32)
    drow = lax.broadcasted_iota(jnp.int32, (128, 128), 0)
    weigh = jnp.where(drow == 0, 1024.0, jnp.where(drow == 1, 32.0, jnp.where(drow == 2, 1.0, 0.0))).astype(BF16)
    ramp = lax.broadcasted_iota(jnp.int32, (1, 128), 1).astype(F32)

    def turn(src, dst_t, dst_i, base):
        rows = src[...].reshape(R, DX)
        for i in range(8):
            dst_t[:, i * 128 : (i + 1) * 128] = rows[i * 128 : (i + 1) * 128, :D].T
        dst_i[...] = jnp.dot(rows[:, D:], weigh, preferred_element_type=F32) - (ramp + base)

    turn(eg, et, icol, first_col)
    for c in cs:
        c.wait()
    m, s = merge([st[0]] + [ra[j] for j in range(7)])
    st[1, 0:8, :] = m
    st[1, 8:16, :] = s
    cs = exchange(st.at[1], rb, s_b.at[0], r_b.at[0], wide_peers)

    for k in (0, 1, 3, 2):
        block = eg2.at[other, add4(alpha, 4 - k)]
        remote(block, block, s_f3.at[k], r_f3.at[k], partner).wait_recv()
    half_w = pl.ds(pl.multiple_of(own_cols, H), H)
    for h in range(2):
        left = eg2[h].reshape(R // 2, DX)[:, :D]
        lb2[h * 512 : (h + 1) * 512, :] = jnp.dot(left, w_ref[:, half_w], preferred_element_type=F32) * LOGIT_SCALE
    for c in cs:
        c.wait()
    m, s = merge([st[1]] + [rb[j] for j in range(7)])
    st[2, 0:8, :] = m
    st[2, 8:16, :] = s
    to_buddy = remote(st.at[2], rc, s_c.at[0], r_c.at[0], buddy_peer)
    to_buddy.start()
    f = jnp.exp(st[0, 0:8, :] - m) / s

    frow = jnp.concatenate([f[i : i + 1, :] for i in range(8)], axis=1)
    part = jnp.dot(split_rows(frow), pb[...], preferred_element_type=F32)
    cm[0] = jnp.sum(part, axis=0, keepdims=True)
    cs = [remote(cm.at[0], cm.at[j], s_m.at[j - 1], r_m.at[j - 1], dp_peers[j - 1]) for j in (1, 2, 3)]
    for c in cs:
        c.start()
    to_cols(acol, f)
    turn(eg2, et2, icol2, first_col + own_cols.astype(F32))
    for c in cs:
        c.wait()
    lr = jnp.log((cm[0] + cm[1] + cm[2] + cm[3]) * classes_over_crops)
    lrow[...] = lr
    lhalf[...] = lrow[:, half_w]

    part = lax.dot_general(split_rows(lr), pb[...], NT, preferred_element_type=F32)
    part = jnp.sum(part, axis=0, keepdims=True)
    for i in range(8):
        qt[0, i : i + 1, :] = part[:, i * 128 : (i + 1) * 128] * f[i : i + 1, :]
    cs = exchange(qt.at[0], qa, s_a.at[1], r_a.at[1], seven_peers)

    to_buddy.wait()
    to_cols(mcol2, rc[0:8, :])
    to_cols(acol2, 1.0 / rc[8:16, :])
    for i in range(4):
        rows = pl.ds(i * 256, 256)
        pb2[rows, :] = jnp.exp(lb2[rows, :] - mcol2[rows, 0:1]).astype(BF16)
    for c in cs:
        c.wait()
    qt[1] = qt[0] + ((qa[0] + qa[1]) + (qa[2] + qa[3])) + ((qa[4] + qa[5]) + qa[6])
    for c in (cs := exchange(qt.at[1], qb, s_b.at[1], r_b.at[1], wide_peers)):
        c.wait()
    qt[2] = qt[1] + ((qb[0] + qb[1]) + (qb[2] + qb[3])) + ((qb[4] + qb[5]) + qb[6])
    to_buddy = remote(qt.at[2], qc, s_c.at[1], r_c.at[1], buddy_peer)
    to_buddy.start()
    to_cols(ccol, f * (1.0 - qt[2]))

    def grad(dst, src, a_ref, c_ref, i_ref, l_ref, first, width):
        def strip(i, _):
            rows = pl.ds(pl.multiple_of(i * 32, 32), 32)
            a = a_ref[rows, :]
            c = c_ref[rows, :]
            hit = i_ref[rows, :]
            for t in range(first // 128, (first + width) // 128):
                cols = pl.ds(t * 128, 128)
                g = src[rows, cols].astype(F32) * (a * l_ref[:, cols] + c)
                g = jnp.where(hit == t * 128.0, g - 1.0, g)
                dst[rows, cols] = g.astype(BF16)
            return 0

        lax.fori_loop(0, R // 32, strip, 0)

    def half_embed(ci):
        rows = pl.ds(pl.multiple_of(ci * 512, 512), 512)
        v = lax.dot_general(gb[rows, :], w_ref[...], NT, preferred_element_type=F32) * LOGIT_SCALE
        xe[ci] = v.reshape(4, 2, 4, 16, D)

    def far(t):
        return remote(pp.at[t], pr.at[t], s_pf.at[t], r_pf.at[t], mate_peer)

    def near(t):
        return remote(pn.at[t], rn.at[t], s_pn.at[t], r_pn.at[t], mate_peer)

    def relay(t, j):
        peer = (far_in, cls) if j == 0 else (far_out, cls)
        return remote(ps.at[t, j], po2.at[t], s_ps.at[t, j], r_ps.at[t], peer)

    def proto(t):
        cols = pl.ds(pl.multiple_of(own_cols + t * CW, CW), CW)
        half = pl.ds(t * CW, CW)
        part = jnp.dot(et[...], gb[:, cols], preferred_element_type=F32)
        part = (part + jnp.dot(et2[...], gb2[:, half], preferred_element_type=F32)) * LOGIT_SCALE
        for k in range(4):
            pf[t, k] = part[k * Q : (k + 1) * Q, :]

        @pl.when(jnp.logical_not(inner))
        def _():
            pp[t, 0] = pf[t, far_in].astype(BF16)
            pp[t, 1] = pf[t, far_out].astype(BF16)
            far(t).start()

        pn[t] = pf[t, mate].astype(BF16)
        near(t).start()

    def settle_far(t):
        @pl.when(inner)
        def _():
            far(t).wait_recv()
            ps[t, 1] = (pf[t, far_out] + pr[t, 1].astype(F32)).astype(BF16)
            relay(t, 1).start()
            ps[t, 0] = (pf[t, far_in] + pr[t, 0].astype(F32)).astype(BF16)
            relay(t, 0).start()

    grad(gb, pb, acol, ccol, icol, lrow, 0, W)
    to_buddy.wait()
    to_cols(ccol2, (1.0 - qc[...]) / rc[8:16, :])
    grad(gb2, pb2, acol2, ccol2, icol2, lhalf, 0, H // 2)
    proto(0)
    proto(1)
    half_embed(other)
    c1 = remote(xe.at[other], xc, s_x1, r_x1, partner)
    c1.start()
    grad(gb2, pb2, acol2, ccol2, icol2, lhalf, H // 2, H // 2)
    proto(2)
    proto(3)
    half_embed(core)
    c1.wait()
    xe[core] = xe[core] + xc[...]
    y1[...] = xe[core].astype(BF16)
    cs = [
        remote(y1.at[add4(beta, k)], xb.at[k - 1], s_x2.at[k - 1], r_x2.at[k - 1], beta_peers[k - 1])
        for k in (1, 2, 3)
    ]
    for c in cs:
        c.start()
    settle_far(0)
    settle_far(1)
    for c in cs:
        c.wait()
    own = xe[core, beta] + xb[0].astype(F32) + xb[1].astype(F32) + xb[2].astype(F32)
    xe[core, beta] = own
    y2[...] = own.astype(BF16)
    cs = []
    for j, (dz, da) in enumerate(SEVEN):
        z2, a2 = seven(dz, da)
        cs.append(remote(y2.at[z2, a2], xa.at[j], s_x3.at[j], r_x3.at[j], seven_peers[j]))
    for c in cs:
        c.start()
    settle_far(2)
    settle_far(3)
    for t in range(NC):
        near(t).wait()
        cols = pl.ds(pl.multiple_of(own_cols + t * CW, CW), CW)
        po_ref[:, cols] = pf[t, dp] + rn[t].astype(F32)
    for c in cs:
        c.wait()
    total = xe[core, beta, zh, alpha]
    for j in range(7):
        total = total + xa[j].astype(F32)
    eo_ref[...] = total
    for t in range(NC):
        relay(t, 0).wait_recv()
        cols = pl.ds(pl.multiple_of(H - own_cols + t * CW, CW), CW)
        po_ref[:, cols] = po2[t].astype(F32)

    @pl.when(inner)
    def _():
        for t in range(NC):
            relay(t, 1).wait_send()
            relay(t, 0).wait_send()

    @pl.when(jnp.logical_not(inner))
    def _():
        for t in range(NC):
            far(t).wait_send()

    for c in sends:
        c.wait_send()


def on_device(classes_over_crops, embeddings, cluster_ids, prototypes):
    vmem = pl.BlockSpec(memory_space=pltpu.VMEM)
    dma = pltpu.SemaphoreType.DMA
    V = pltpu.VMEM
    scratch = [
        V((D, W), BF16),
        V((2, 4, 2, 4, 16, DX), BF16),
        V((2, 4, 2, 4, 16, DX), BF16),
        V((R, W), BF16),
        V((R, H), F32),
        V((R, H), BF16),
    ] + [V((R, 128), F32)] * 9 + [
        V((D, R), BF16),
        V((D, R), BF16),
        V((R, W), BF16),
        V((R, H), BF16),
        V((3, 16, 128), F32),
        V((7, 16, 128), F32),
        V((7, 16, 128), F32),
        V((16, 128), F32),
        V((4, 1, W), F32),
        V((1, W), F32),
        V((1, H), F32),
        V((3, 8, 128), F32),
        V((7, 8, 128), F32),
        V((7, 8, 128), F32),
        V((8, 128), F32),
        V((NC, 4, Q, CW), F32),
        V((NC, 2, Q, CW), BF16),
        V((NC, 2, Q, CW), BF16),
        V((NC, Q, CW), BF16),
        V((NC, Q, CW), BF16),
        V((NC, 2, Q, CW), BF16),
        V((NC, Q, CW), BF16),
        V((2, 4, 2, 4, 16, D), F32),
        V((4, 2, 4, 16, D), F32),
        V((4, 2, 4, 16, D), BF16),
        V((3, 2, 4, 16, D), BF16),
        V((2, 4, 16, D), BF16),
        V((7, 16, D), BF16),
        dma,
        dma((7,)), dma((7,)), dma((3,)), dma((3,)), dma((4,)), dma((4,)), dma, dma, dma((3,)), dma((3,)), dma((4,)), dma((4,)),
        dma((2, 7)), dma((2, 7)), dma((2, 7)), dma((2, 7)), dma((2,)), dma((2,)),
        dma((3,)), dma((3,)),
        dma((NC,)), dma((NC,)), dma((NC,)), dma((NC,)), dma((NC, 2)), dma((NC,)),
        dma, dma, dma((3,)), dma((3,)), dma((7,)), dma((7,)),
    ]
    halves = pl.pallas_call(
        functools.partial(kernel, classes_over_crops),
        out_shape=(jax.ShapeDtypeStruct((16, D), F32), jax.ShapeDtypeStruct((Q, W), F32)),
        in_specs=[pl.BlockSpec(memory_space=pltpu.SMEM), vmem, pl.BlockSpec(memory_space=pl.ANY)],
        out_specs=(vmem, vmem),
        scratch_shapes=scratch,
        compiler_params=pltpu.CompilerParams(
            collective_id=0, has_side_effects=True, vmem_limit_bytes=56 * 2**20
        ),
    )(cluster_ids, embeddings, prototypes)

    any_space = pl.BlockSpec(memory_space=pl.ANY)

    def hand_over(a_ref, b_ref, a_out, b_out, sems):
        a_out[...] = a_ref[...]
        b_out[...] = b_ref[...]

    return pl.pallas_call(
        hand_over,
        out_shape=(jax.ShapeDtypeStruct((16, D), F32), jax.ShapeDtypeStruct((Q, W), F32)),
        in_specs=[vmem] * 2,
        out_specs=(vmem,) * 2,
        scratch_shapes=[dma((2,))],
    )(*halves)


def solution(mesh):
    placed = (P(("dp", "cls"), None), P(("dp", "cls")), P(None, "cls"))
    return jax.shard_map(
        functools.partial(on_device, 131072 / 4096),
        mesh=mesh,
        in_specs=placed,
        out_specs=(P(("dp", "cls"), None), P("dp", "cls")),
        check_vma=False,
    )
```

```python
import functools

import jax
import jax.numpy as jnp
from jax import lax
from jax.experimental import pallas as pl
from jax.experimental.pallas import tpu as pltpu
from jax.sharding import PartitionSpec as P

LOGIT_SCALE = 10.0
MESH = pl.DeviceIdType.MESH
F32 = jnp.float32
BF16 = jnp.bfloat16

D = 384
DX = 512
W = 2048
R = 1024
H = W // 2
NC = 4
CW = H // NC
Q = D // 4
NT = (((1,), (1,)), ((), ()))
SEVEN = [(1, 2), (1, 1), (1, 3), (1, 0), (0, 2), (0, 1), (0, 3)]


def split_rows(v):
    hi = v.astype(BF16)
    r1 = v - hi.astype(F32)
    mid = r1.astype(BF16)
    lo = (r1 - mid.astype(F32)).astype(BF16)
    row = lax.broadcasted_iota(jnp.int32, (16, v.shape[1]), 0)
    zero = jnp.zeros((16, v.shape[1]), F32)
    out = jnp.where(row == 0, hi.astype(F32), zero)
    out = jnp.where(row == 1, mid.astype(F32), out)
    out = jnp.where(row == 2, lo.astype(F32), out)
    return out.astype(BF16)


def kernel(classes_over_crops, id_ref, e_ref, w_hbm, eo_ref, po_ref,
           w_ref, eg, eg2, pb, lb2, pb2, mcol, scol, acol, ccol, icol, acol2, ccol2, icol2, mcol2, et, et2, gb, gb2,
           st, ra, rb, rc, cm, lrow, lhalf, qt, qa, qb, qc, pf, pp, pr, pn, rn, ps, po2,
           xe, xc, y1, xb, y2, xa,
           s_w, s_e1, r_e1, s_e2, r_e2, s_e3, r_e3, s_f1, r_f1, s_f2, r_f2, s_f3, r_f3,
           s_a, r_a, s_b, r_b, s_c, r_c, s_m, r_m,
           s_pf, r_pf, s_pn, r_pn, s_ps, r_ps, s_x1, r_x1, s_x2, r_x2, s_x3, r_x3):
    dp = lax.axis_index("dp")
    cls = lax.axis_index("cls")
    core = lax.rem(cls, 2)
    x = lax.rem(cls // 2, 4)
    zh = lax.rem(cls // 8, 2)
    y = cls // 16
    other = 1 - core
    alpha = y * other + x * core
    beta = x * other + y * core
    pair = dp // 2
    mate = dp + 1 - 2 * lax.rem(dp, 2)
    inner = jnp.logical_or(dp == 1, dp == 2)
    far_in = 2 - pair
    far_out = 3 - 3 * pair
    own_cols = pair * H

    def at(zz, aa, bb):
        yy = aa * other + bb * core
        xx = bb * other + aa * core
        return (dp, ((yy * 2 + zz) * 4 + xx) * 2 + core)

    def add4(v, k):
        return lax.rem(v + k, 4)

    def seven(dz, da):
        return lax.rem(zh + dz, 2), add4(alpha, da)

    twin = cls + 1 - 2 * core
    partner = (dp, twin)
    buddy = add4(dp, 2)
    mate_peer = (mate, cls)
    buddy_peer = (buddy, cls)
    dp_peers = [(add4(dp, j), cls) for j in (1, 2, 3)]
    beta_peers = [at(zh, alpha, add4(beta, k)) for k in (1, 2, 3)]
    seven_peers = [at(*seven(dz, da), beta) for dz, da in SEVEN]

    def cross(peer):
        return (dp, peer[1] + 1 - 2 * core)

    wide_peers = [cross(beta_peers[1]), beta_peers[1], cross(beta_peers[0]), cross(beta_peers[2])]
    wide_peers = wide_peers + [beta_peers[0], beta_peers[2], partner]
    wide_from = [cross(at(zh, add4(alpha, k), beta)) for k in (1, 2, 3)]

    barrier = pltpu.get_barrier_semaphore()
    everyone = seven_peers + dp_peers + wide_from + beta_peers + [partner]
    for peer in everyone:
        pl.semaphore_signal(barrier, inc=1, device_id=peer, device_id_type=MESH)
    load = pltpu.make_async_copy(w_hbm, w_ref, s_w)
    load.start()

    lane = lax.broadcasted_iota(jnp.int32, (16, 128), 1)
    line = lax.broadcasted_iota(jnp.int32, (16, 128), 0)
    ids = jnp.zeros((16, 128), jnp.int32)
    for i in range(16):
        ids = jnp.where(line == i, id_ref[i], ids)
    digits = jnp.where(lane == 0, ids >> 10, jnp.where(lane == 1, (ids >> 5) & 31, jnp.where(lane == 2, ids & 31, 0)))
    eg[core, beta, zh, alpha, :, :D] = e_ref[...]
    eg[core, beta, zh, alpha, :, D:] = digits.astype(F32).astype(BF16)

    pl.semaphore_wait(barrier, len(everyone))

    def remote(src, dst, ssem, rsem, peer):
        return pltpu.make_async_remote_copy(
            src_ref=src, dst_ref=dst, send_sem=ssem, recv_sem=rsem, device_id=peer, device_id_type=MESH
        )

    sends = []

    def post(src, dst, ssem, rsem, peer):
        c = remote(src, dst, ssem, rsem, peer)
        c.start()
        sends.append(c)

    mine = eg.at[core, beta, zh, alpha]
    for j, peer in enumerate(seven_peers):
        post(mine, mine, s_e1.at[j], r_e1.at[j], peer)
    for j, (dz, da) in enumerate(SEVEN):
        block = eg.at[core, beta, lax.rem(zh + dz, 2), add4(alpha, 4 - da)]
        remote(block, block, s_e1.at[j], r_e1.at[j], seven_peers[j]).wait_recv()
    row = eg.at[core, beta]
    for k in (1, 0, 2):
        post(row, row, s_e2.at[k], r_e2.at[k], beta_peers[k])
    post(row, row, s_e3.at[0], r_e3.at[0], partner)
    row2 = eg2.at[core, beta]
    post(row, row2, s_f1, r_f1, buddy_peer)
    load.wait()
    for k in (1, 3, 2):
        b = add4(beta, 4 - k)
        block = eg.at[core, b]
        remote(block, block, s_e2.at[k - 1], r_e2.at[k - 1], beta_peers[k - 1]).wait_recv()
        post(block, block, s_e3.at[k], r_e3.at[k], partner)

    def half_logits(ci):
        for h in range(2):
            left = eg[ci, 2 * h : 2 * h + 2].reshape(256, DX)[:, :D]
            there = pl.ds(pl.multiple_of(ci * (R // 2) + h * 256, 256), 256)
            v = jnp.dot(left, w_ref[...], preferred_element_type=F32) * LOGIT_SCALE
            m = jnp.max(v, axis=1, keepdims=True)
            p = jnp.exp(v - m)
            s = jnp.sum(p, axis=1, keepdims=True)
            pb[there, :] = p.astype(BF16)
            mcol[there, :] = jnp.broadcast_to(m, (256, 128))
            scol[there, :] = jnp.broadcast_to(s, (256, 128))

    half_logits(core)
    for k in (0, 1, 3, 2):
        block = eg.at[other, add4(alpha, 4 - k)]
        remote(block, block, s_e3.at[k], r_e3.at[k], partner).wait_recv()
    half_logits(other)

    remote(row2, row2, s_f1, r_f1, buddy_peer).wait_recv()
    for k, peer in enumerate(beta_peers):
        post(row2, row2, s_f2.at[k], r_f2.at[k], peer)
    post(row2, row2, s_f3.at[0], r_f3.at[0], partner)

    eye = lax.broadcasted_iota(jnp.int32, (128, 128), 0) == lax.broadcasted_iota(jnp.int32, (128, 128), 1)

    def to_line(cols):
        return jnp.sum(jnp.where(eye, cols, 0.0), axis=0, keepdims=True)

    def to_cols(dst, lines):
        for i in range(8):
            dst[i * 128 : (i + 1) * 128, :] = jnp.broadcast_to(lines[i : i + 1, :], (128, 128)).T

    for i in range(8):
        here = pl.ds(i * 128, 128)
        st[0, i : i + 1, :] = to_line(mcol[here, :])
        st[0, 8 + i : 9 + i, :] = to_line(scol[here, :])

    def exchange(src, dst, ssem, rsem, peers):
        cs = [remote(src, dst.at[j], ssem.at[j], rsem.at[j], peer) for j, peer in enumerate(peers)]
        for c in cs:
            c.start()
        return cs

    def merge(parts):
        m = parts[0][0:8, :]
        for v in parts[1:]:
            m = jnp.maximum(m, v[0:8, :])
        s = parts[0][8:16, :] * jnp.exp(parts[0][0:8, :] - m)
        for v in parts[1:]:
            s = s + v[8:16, :] * jnp.exp(v[0:8, :] - m)
        return m, s

    cs = exchange(st.at[0], ra, s_a.at[0], r_a.at[0], seven_peers)

    for k in (1, 3, 2):
        block = eg2.at[core, add4(beta, 4 - k)]
        remote(block, block, s_f2.at[k - 1], r_f2.at[k - 1], beta_peers[k - 1]).wait_recv()
        post(block, block, s_f3.at[k], r_f3.at[k], partner)

    first_col = (cls * W).astype(F32)
    drow = lax.broadcasted_iota(jnp.int32, (128, 128), 0)
    weigh = jnp.where(drow == 0, 1024.0, jnp.where(drow == 1, 32.0, jnp.where(drow == 2, 1.0, 0.0))).astype(BF16)
    ramp = lax.broadcasted_iota(jnp.int32, (1, 128), 1).astype(F32)

    def turn(src, dst_t, dst_i, base):
        rows = src[...].reshape(R, DX)
        for i in range(8):
            dst_t[:, i * 128 : (i + 1) * 128] = rows[i * 128 : (i + 1) * 128, :D].T
        dst_i[...] = jnp.dot(rows[:, D:], weigh, preferred_element_type=F32) - (ramp + base)

    turn(eg, et, icol, first_col)
    for c in cs:
        c.wait()
    m, s = merge([st[0]] + [ra[j] for j in range(7)])
    st[1, 0:8, :] = m
    st[1, 8:16, :] = s
    cs = exchange(st.at[1], rb, s_b.at[0], r_b.at[0], wide_peers)

    for k in (0, 1, 3, 2):
        block = eg2.at[other, add4(alpha, 4 - k)]
        remote(block, block, s_f3.at[k], r_f3.at[k], partner).wait_recv()
    half_w = pl.ds(pl.multiple_of(own_cols, H), H)
    for h in range(2):
        left = eg2[h].reshape(R // 2, DX)[:, :D]
        lb2[h * 512 : (h + 1) * 512, :] = jnp.dot(left, w_ref[:, half_w], preferred_element_type=F32) * LOGIT_SCALE
    for c in cs:
        c.wait()
    m, s = merge([st[1]] + [rb[j] for j in range(7)])
    st[2, 0:8, :] = m
    st[2, 8:16, :] = s
    to_buddy = remote(st.at[2], rc, s_c.at[0], r_c.at[0], buddy_peer)
    to_buddy.start()
    f = jnp.exp(st[0, 0:8, :] - m) / s

    frow = jnp.concatenate([f[i : i + 1, :] for i in range(8)], axis=1)
    part = jnp.dot(split_rows(frow), pb[...], preferred_element_type=F32)
    cm[0] = jnp.sum(part, axis=0, keepdims=True)
    cs = [remote(cm.at[0], cm.at[j], s_m.at[j - 1], r_m.at[j - 1], dp_peers[j - 1]) for j in (1, 2, 3)]
    for c in cs:
        c.start()
    to_cols(acol, f)
    turn(eg2, et2, icol2, first_col + own_cols.astype(F32))
    for c in cs:
        c.wait()
    lr = jnp.log((cm[0] + cm[1] + cm[2] + cm[3]) * classes_over_crops)
    lrow[...] = lr
    lhalf[...] = lrow[:, half_w]

    part = lax.dot_general(split_rows(lr), pb[...], NT, preferred_element_type=F32)
    part = jnp.sum(part, axis=0, keepdims=True)
    for i in range(8):
        qt[0, i : i + 1, :] = part[:, i * 128 : (i + 1) * 128] * f[i : i + 1, :]
    cs = exchange(qt.at[0], qa, s_a.at[1], r_a.at[1], seven_peers)

    to_buddy.wait()
    to_cols(mcol2, rc[0:8, :])
    to_cols(acol2, 1.0 / rc[8:16, :])
    for i in range(4):
        rows = pl.ds(i * 256, 256)
        pb2[rows, :] = jnp.exp(lb2[rows, :] - mcol2[rows, 0:1]).astype(BF16)
    for c in cs:
        c.wait()
    qt[1] = qt[0] + ((qa[0] + qa[1]) + (qa[2] + qa[3])) + ((qa[4] + qa[5]) + qa[6])
    for c in (cs := exchange(qt.at[1], qb, s_b.at[1], r_b.at[1], wide_peers)):
        c.wait()
    qt[2] = qt[1] + ((qb[0] + qb[1]) + (qb[2] + qb[3])) + ((qb[4] + qb[5]) + qb[6])
    to_buddy = remote(qt.at[2], qc, s_c.at[1], r_c.at[1], buddy_peer)
    to_buddy.start()
    to_cols(ccol, f * (1.0 - qt[2]))

    def grad(dst, src, a_ref, c_ref, i_ref, l_ref, first, width):
        def strip(i, _):
            rows = pl.ds(pl.multiple_of(i * 32, 32), 32)
            a = a_ref[rows, :]
            c = c_ref[rows, :]
            hit = i_ref[rows, :]
            for t in range(first // 128, (first + width) // 128):
                cols = pl.ds(t * 128, 128)
                g = src[rows, cols].astype(F32) * (a * l_ref[:, cols] + c)
                g = jnp.where(hit == t * 128.0, g - 1.0, g)
                dst[rows, cols] = g.astype(BF16)
            return 0

        lax.fori_loop(0, R // 32, strip, 0)

    def half_embed(ci):
        rows = pl.ds(pl.multiple_of(ci * 512, 512), 512)
        v = lax.dot_general(gb[rows, :], w_ref[...], NT, preferred_element_type=F32) * LOGIT_SCALE
        xe[ci] = v.reshape(4, 2, 4, 16, D)

    def far(t):
        return remote(pp.at[t], pr.at[t], s_pf.at[t], r_pf.at[t], mate_peer)

    def near(t):
        return remote(pn.at[t], rn.at[t], s_pn.at[t], r_pn.at[t], mate_peer)

    def relay(t, j):
        peer = (far_in, cls) if j == 0 else (far_out, cls)
        return remote(ps.at[t, j], po2.at[t], s_ps.at[t, j], r_ps.at[t], peer)

    def proto(t):
        cols = pl.ds(pl.multiple_of(own_cols + t * CW, CW), CW)
        half = pl.ds(t * CW, CW)
        part = jnp.dot(et[...], gb[:, cols], preferred_element_type=F32)
        part = (part + jnp.dot(et2[...], gb2[:, half], preferred_element_type=F32)) * LOGIT_SCALE
        for k in range(4):
            pf[t, k] = part[k * Q : (k + 1) * Q, :]

        @pl.when(jnp.logical_not(inner))
        def _():
            pp[t, 0] = pf[t, far_in].astype(BF16)
            pp[t, 1] = pf[t, far_out].astype(BF16)
            far(t).start()

        pn[t] = pf[t, mate].astype(BF16)
        near(t).start()

    def settle_far(t):
        @pl.when(inner)
        def _():
            far(t).wait_recv()
            ps[t, 1] = (pf[t, far_out] + pr[t, 1].astype(F32)).astype(BF16)
            relay(t, 1).start()
            ps[t, 0] = (pf[t, far_in] + pr[t, 0].astype(F32)).astype(BF16)
            relay(t, 0).start()

    grad(gb, pb, acol, ccol, icol, lrow, 0, W)
    to_buddy.wait()
    to_cols(ccol2, (1.0 - qc[...]) / rc[8:16, :])
    grad(gb2, pb2, acol2, ccol2, icol2, lhalf, 0, H // 2)
    proto(0)
    proto(1)
    half_embed(other)
    c1 = remote(xe.at[other], xc, s_x1, r_x1, partner)
    c1.start()
    grad(gb2, pb2, acol2, ccol2, icol2, lhalf, H // 2, H // 2)
    proto(2)
    proto(3)
    half_embed(core)
    c1.wait()
    xe[core] = xe[core] + xc[...]
    y1[...] = xe[core].astype(BF16)
    cs = [
        remote(y1.at[add4(beta, k)], xb.at[k - 1], s_x2.at[k - 1], r_x2.at[k - 1], beta_peers[k - 1])
        for k in (2, 1, 3)
    ]
    for c in cs:
        c.start()
    settle_far(0)
    settle_far(1)
    for c in cs:
        c.wait()
    own = xe[core, beta] + xb[0].astype(F32) + xb[1].astype(F32) + xb[2].astype(F32)
    xe[core, beta] = own
    y2[...] = own.astype(BF16)
    cs = []
    for j, (dz, da) in enumerate(SEVEN):
        z2, a2 = seven(dz, da)
        cs.append(remote(y2.at[z2, a2], xa.at[j], s_x3.at[j], r_x3.at[j], seven_peers[j]))
    for c in cs:
        c.start()
    settle_far(2)
    settle_far(3)
    for t in range(NC):
        near(t).wait()
        cols = pl.ds(pl.multiple_of(own_cols + t * CW, CW), CW)
        po_ref[:, cols] = pf[t, dp] + rn[t].astype(F32)
    for c in cs:
        c.wait()
    total = xe[core, beta, zh, alpha]
    for j in range(7):
        total = total + xa[j].astype(F32)
    eo_ref[...] = total
    for t in range(NC):
        relay(t, 0).wait_recv()
        cols = pl.ds(pl.multiple_of(H - own_cols + t * CW, CW), CW)
        po_ref[:, cols] = po2[t].astype(F32)

    @pl.when(inner)
    def _():
        for t in range(NC):
            relay(t, 1).wait_send()
            relay(t, 0).wait_send()

    @pl.when(jnp.logical_not(inner))
    def _():
        for t in range(NC):
            far(t).wait_send()

    for c in sends:
        c.wait_send()


def on_device(classes_over_crops, embeddings, cluster_ids, prototypes):
    vmem = pl.BlockSpec(memory_space=pltpu.VMEM)
    dma = pltpu.SemaphoreType.DMA
    V = pltpu.VMEM
    scratch = [
        V((D, W), BF16),
        V((2, 4, 2, 4, 16, DX), BF16),
        V((2, 4, 2, 4, 16, DX), BF16),
        V((R, W), BF16),
        V((R, H), F32),
        V((R, H), BF16),
    ] + [V((R, 128), F32)] * 9 + [
        V((D, R), BF16),
        V((D, R), BF16),
        V((R, W), BF16),
        V((R, H), BF16),
        V((3, 16, 128), F32),
        V((7, 16, 128), F32),
        V((7, 16, 128), F32),
        V((16, 128), F32),
        V((4, 1, W), F32),
        V((1, W), F32),
        V((1, H), F32),
        V((3, 8, 128), F32),
        V((7, 8, 128), F32),
        V((7, 8, 128), F32),
        V((8, 128), F32),
        V((NC, 4, Q, CW), F32),
        V((NC, 2, Q, CW), BF16),
        V((NC, 2, Q, CW), BF16),
        V((NC, Q, CW), BF16),
        V((NC, Q, CW), BF16),
        V((NC, 2, Q, CW), BF16),
        V((NC, Q, CW), BF16),
        V((2, 4, 2, 4, 16, D), F32),
        V((4, 2, 4, 16, D), F32),
        V((4, 2, 4, 16, D), BF16),
        V((3, 2, 4, 16, D), BF16),
        V((2, 4, 16, D), BF16),
        V((7, 16, D), BF16),
        dma,
        dma((7,)), dma((7,)), dma((3,)), dma((3,)), dma((4,)), dma((4,)), dma, dma, dma((3,)), dma((3,)), dma((4,)), dma((4,)),
        dma((2, 7)), dma((2, 7)), dma((2, 7)), dma((2, 7)), dma((2,)), dma((2,)),
        dma((3,)), dma((3,)),
        dma((NC,)), dma((NC,)), dma((NC,)), dma((NC,)), dma((NC, 2)), dma((NC,)),
        dma, dma, dma((3,)), dma((3,)), dma((7,)), dma((7,)),
    ]
    halves = pl.pallas_call(
        functools.partial(kernel, classes_over_crops),
        out_shape=(jax.ShapeDtypeStruct((16, D), F32), jax.ShapeDtypeStruct((Q, W), F32)),
        in_specs=[pl.BlockSpec(memory_space=pltpu.SMEM), vmem, pl.BlockSpec(memory_space=pl.ANY)],
        out_specs=(vmem, vmem),
        scratch_shapes=scratch,
        compiler_params=pltpu.CompilerParams(
            collective_id=0, has_side_effects=True, vmem_limit_bytes=56 * 2**20
        ),
    )(cluster_ids, embeddings, prototypes)

    any_space = pl.BlockSpec(memory_space=pl.ANY)

    def hand_over(a_ref, b_ref, a_out, b_out, sems):
        a_out[...] = a_ref[...]
        b_out[...] = b_ref[...]

    return pl.pallas_call(
        hand_over,
        out_shape=(jax.ShapeDtypeStruct((16, D), F32), jax.ShapeDtypeStruct((Q, W), F32)),
        in_specs=[vmem] * 2,
        out_specs=(vmem,) * 2,
        scratch_shapes=[dma((2,))],
    )(*halves)


def solution(mesh):
    placed = (P(("dp", "cls"), None), P(("dp", "cls")), P(None, "cls"))
    return jax.shard_map(
        functools.partial(on_device, 131072 / 4096),
        mesh=mesh,
        in_specs=placed,
        out_specs=(P(("dp", "cls"), None), P("dp", "cls")),
        check_vma=False,
    )
```
